256 devices in a mesh: dp: 4 (over x_hi, core), seq: 64 (over x_lo, y, z).
Axes of the slice: x: 4 (x_hi: 2, x_lo: 2; x = x_hi * 2 + x_lo), y: 4, z: 8, core: 2. Of those that a mesh axis runs over, the one named last changes fastest.
Arguments:
- ids: int32 [4, 8192], P('dp', 'seq'), may hold values from 0 to 511
- embed: bfloat16 [512, 2048], replicated, may hold values from -6 to 6
- weight: bfloat16 [2048, 2048], P('seq'), may hold values from -0.125 to 0.125
- filters: float32 [2048, 8192], P('seq'), may hold values from -4 to 4
- out_grad: bfloat16 [4, 8192, 2048], P('dp', 'seq'), may hold values from -6 to 6
- momentum: float32 [4, 2048, 2048], P('dp', 'seq'), may hold values from -8 to 8
- feedback: float32 [4, 2048, 2048], P('dp', 'seq'), may hold values from -4 to 4
Outputs:
- output: bfloat16 [4, 8192, 2048], P('dp', 'seq')
- new_momentum: float32 [4, 2048, 2048], P('dp', 'seq')
- new_feedback: float32 [4, 2048, 2048], P('dp', 'seq')
- new_weight: bfloat16 [2048, 2048], P('seq')
The draws below stay inside these ranges and needn't reach their ends.
All inputs are finite; a program needn't handle non-finite values. Where the reference program divides by a largest or mean magnitude, that divisor is 1e-20 or more.
Results may differ from the reference program's by a relative error of at most 0.008.
Values may be sent and summed in bfloat16 or wider, within the bound.
No kernel may reach another device: no remote copies, remote signals or barrier semaphores. Data moves between devices by JAX's collectives and lax.ppermute only.
A program may use at most 128 MiB of HBM per device.

```python
import math
import jax
import jax.numpy as jnp
import numpy as np
from jax import lax

MIXER_WIDTH = 2048
VOCAB = 512
CONTEXT_SPAN = 8192
SEQS = 4
N_DP = 4


def draw_filters(key, part):
    key = jax.random.fold_in(key, 11)
    key_span, key_rough, random_seed_slot, key_drop = jax.random.split(key, 4)
    training_iterations = lax.iota(jnp.float32, CONTEXT_SPAN)[None, :]
    kernel_widths = jnp.exp(jax.random.uniform(key_span, (MIXER_WIDTH, 1), jnp.float32, math.log(30.0), math.log(4 * CONTEXT_SPAN)))
    rough = jnp.clip(jax.random.normal(key_rough, (MIXER_WIDTH, CONTEXT_SPAN), jnp.float32), -4.0, 4.0)
    impulse_index = jax.random.randint(random_seed_slot, (MIXER_WIDTH, 1), 0, CONTEXT_SPAN)
    kept_coordinates = jax.random.uniform(key_drop, (MIXER_WIDTH, 1), jnp.float32, 0.5, 0.8)
    fading_profile = jnp.exp(-training_iterations / kernel_widths) * jnp.where(training_iterations >= impulse_index.astype(jnp.float32), kept_coordinates, 1.0)
    energy = (1.0 - jnp.exp(-2.0 * CONTEXT_SPAN / kernel_widths)) / (1.0 - jnp.exp(-2.0 / kernel_widths))
    return rough * fading_profile / jnp.sqrt(energy)


def draw_momentum(key, part):
    key = jax.random.fold_in(key, 23)
    key_rows, key_cols, key_base = jax.random.split(key, 3)
    row_scale = jnp.exp(jax.random.uniform(key_rows, (N_DP, MIXER_WIDTH, 1), jnp.float32, 0.0, math.log(10.0)))
    col_scale = jnp.exp(jax.random.uniform(key_cols, (N_DP, 1, MIXER_WIDTH), jnp.float32, 0.0, math.log(10.0)))
    base = jnp.clip(jax.random.normal(key_base, (N_DP, MIXER_WIDTH, MIXER_WIDTH), jnp.float32), -4.0, 4.0)
    return 0.02 * base * row_scale * col_scale


def place_ends(entries, key, least, high):
    dims = entries.shape
    spot = [jax.random.randint(jax.random.fold_in(key, axis), (), 0, dims[axis]) for axis in range(len(dims))]
    entries = entries.at[tuple(spot)].set(least)
    longest = dims.index(max(dims))
    spot[longest] = (spot[longest] + 1) % dims[longest]
    return entries.at[tuple(spot)].set(high)


def shard_levels(own_key, shape, cuts, least, high):
    level, own = 1.0, jax.random.fold_in(own_key, 6)
    for axis_at, blocks in cuts:
        steps = jnp.exp(jax.random.uniform(jax.random.fold_in(own, axis_at), (blocks,), jnp.float32, least / len(cuts), high / len(cuts)))
        level = level * jnp.repeat(steps, shape[axis_at] // blocks).reshape([-1 if axis == axis_at else 1 for axis in range(len(shape))])
    return level


def rank_table(count, skew):
    weights = [(1 << 20) // math.isqrt(rank ** skew) + 1 for rank in range(1, count + 1)]
    spread = 1 + sum(weights) // (1 << 30)
    return np.cumsum(np.array([max(1, weight // spread) for weight in weights]))


def ranked(stream_key, extent, count, skew):
    table = rank_table(count, skew)
    pick = jax.random.randint(jax.random.fold_in(stream_key, 1), extent, 0, int(table[count - 1]))
    standing = jnp.searchsorted(jnp.asarray(table, jnp.int32), pick, side="right")
    return jax.random.permutation(jax.random.fold_in(stream_key, 2), count)[standing].astype(jnp.int32)


def centred(rng, extent, width, most, shards=(), kind=jnp.bfloat16):
    result = width * jax.random.normal(rng, extent, jnp.float32)
    if shards:
        result = result * shard_levels(rng, extent, shards, -0.22, 0.18)
    return jnp.clip(result, -most, most).astype(kind)


def setup_inputs(seed: int = 0) -> dict:
    key_of = jax.random.split(jax.random.key(seed), 8)
    return {
        "ids": place_ends(ranked(key_of[0], (SEQS, CONTEXT_SPAN), VOCAB, 2), jax.random.fold_in(key_of[0], 3), 0, VOCAB - 1).astype(jnp.int32),
        "embed": centred(key_of[1], (VOCAB, MIXER_WIDTH), 1.0, 6.0),
        "weight": centred(key_of[2], (MIXER_WIDTH, MIXER_WIDTH), MIXER_WIDTH ** -0.5, 0.125, ((0, 64),)),
        "filters": draw_filters(jax.random.fold_in(key_of[7], 71), 0),
        "out_grad": centred(key_of[4], (SEQS, CONTEXT_SPAN, MIXER_WIDTH), 1.0, 6.0, ((0, 4), (1, 64))),
        "momentum": draw_momentum(jax.random.fold_in(key_of[7], 71), 0),
        "feedback": centred(key_of[6], (SEQS, MIXER_WIDTH, MIXER_WIDTH), 0.3, 4.0, ((0, 4), (1, 64)), jnp.float32),
    }


def causal_filter(signal, spectrum, length):
    padded = jnp.fft.rfft(signal, n=2 * length, axis=0)
    return jnp.fft.irfft(padded * spectrum, n=2 * length, axis=0)[:length]

def reference(ids, embed, weight, filters, out_grad, momentum, feedback):
    spectrum = jnp.fft.rfft(filters, n=2 * CONTEXT_SPAN, axis=1).T
    outputs = []
    moments = []
    residues = []
    summed = jnp.zeros((MIXER_WIDTH, MIXER_WIDTH), jnp.float32)
    for replica in range(N_DP):
        inputs = embed[ids[replica]]
        projected = jnp.dot(inputs, weight, preferred_element_type=jnp.float32).astype(jnp.bfloat16)
        convolved = causal_filter(projected.astype(jnp.float32), spectrum, CONTEXT_SPAN).astype(jnp.bfloat16)
        outputs.append((inputs.astype(jnp.float32) * convolved.astype(jnp.float32)).astype(jnp.bfloat16))
        upstream = (out_grad[replica].astype(jnp.float32) * inputs.astype(jnp.float32)).astype(jnp.bfloat16)
        downstream = causal_filter(upstream.astype(jnp.float32), jnp.conj(spectrum), CONTEXT_SPAN).astype(jnp.bfloat16)
        gradient = jnp.dot(inputs.T, downstream, preferred_element_type=jnp.float32) * (1.0 / math.sqrt(CONTEXT_SPAN))
        updated = 0.9 * momentum[replica] + 0.1 * gradient
        total = updated + feedback[replica]
        scale = lax.optimization_barrier(jnp.mean(jnp.abs(total), axis=1, keepdims=True)) + 1e-06
        quantized = (scale * jnp.clip(total / scale, -1.0, 1.0)).astype(jnp.bfloat16)
        residues.append(total - quantized.astype(jnp.float32))
        moments.append(updated)
        summed = summed + quantized.astype(jnp.float32)
    average = summed / N_DP
    new_weight = (weight.astype(jnp.float32) - 0.02 * average).astype(jnp.bfloat16)
    return (jnp.stack(outputs), jnp.stack(moments), jnp.stack(residues), new_weight)
```

```python
import functools
import math

import jax
import jax.numpy as jnp
import numpy as np
from jax import lax
from jax.experimental import pallas as pl
from jax.experimental.pallas import tpu as pltpu
from jax.sharding import PartitionSpec as P

momentum_keep = 0.9
step_rate = 0.02
tiny_shift = 1e-06

F32 = jnp.float32
BF16 = jnp.bfloat16
LANES = 128
GROUP = 8
HALVES = 4
SIDE = 32
VMEM_LIMIT = 44 * 1024 * 1024


def split_const(table):
    high = np.asarray(table, np.float32).astype(BF16)
    low = (table - high.astype(np.float64)).astype(np.float32).astype(BF16)
    return high, low


def transform_tables(outer, inner):
    total = outer * inner
    freq = np.arange(outer)[:, None] + 0.25
    first = np.exp(-2j * np.pi * freq * np.arange(outer)[None, :] / outer)
    twist = np.exp(-2j * np.pi * freq * np.arange(inner)[None, :] / total)
    second = np.exp(
        -2j * np.pi * (np.arange(inner)[:, None] * np.arange(inner)[None, :] % inner) / inner
    )
    stage = np.concatenate([first.real, first.imag], axis=0)
    high, low = split_const(stage)
    back_high, back_low = split_const(stage.T)
    real, imag = second.real, second.imag
    mix = np.block([[real, imag], [-imag, real]])
    unmix = np.block([[real, -imag], [imag, real]])
    return {
        "exact": np.concatenate([high, low], axis=1),
        "wide": np.concatenate([high, high, low], axis=1),
        "back": np.concatenate([back_high, back_high, back_low], axis=1),
        "twist": np.concatenate([twist.real, twist.imag], axis=1).astype(np.float32),
        "mix": np.stack(split_const(mix)),
        "unmix": np.stack(split_const(unmix)),
    }


def mm(left, right):
    return jnp.dot(left, right, preferred_element_type=F32)


def halves(values):
    high = values.astype(BF16)
    return high, (values - high.astype(F32)).astype(BF16)


def mm_wide(values, table_ref):
    rows = values.shape[0]
    high, low = halves(values)
    both = mm(jnp.concatenate([high, low], axis=0), table_ref[0])
    return both[:rows] + both[rows:] + mm(high, table_ref[1])


def spread(columns, stage_ref, twist_ref, exact):
    real_twist = twist_ref[:, :LANES]
    imag_twist = twist_ref[:, LANES:]
    outer = real_twist.shape[0]
    rows = []
    for first in range(0, len(columns), 2):
        pair = jnp.concatenate(columns[first : first + 2], axis=1)
        if exact:
            high = pair.astype(BF16)
            stack = jnp.concatenate([high, high], axis=0)
        else:
            high, low = halves(pair)
            stack = jnp.concatenate([high, low, high], axis=0)
        grid = mm(stage_ref[...], stack)
        for which in range(2):
            lane = slice(which * LANES, (which + 1) * LANES)
            real = grid[:outer, lane]
            imag = grid[outer:, lane]
            rows.append(
                jnp.concatenate(
                    [
                        real * real_twist - imag * imag_twist,
                        real * imag_twist + imag * real_twist,
                    ],
                    axis=1,
                )
            )
    return jnp.concatenate(rows, axis=0)


def gather_back(spectrum, back_ref, twist_ref):
    real_twist = twist_ref[:, :LANES]
    imag_twist = twist_ref[:, LANES:]
    outer = real_twist.shape[0]
    count = spectrum.shape[0] // outer
    turned = []
    for which in range(count):
        real = spectrum[which * outer : (which + 1) * outer, :LANES]
        imag = spectrum[which * outer : (which + 1) * outer, LANES:]
        turned.append(
            jnp.concatenate(
                [
                    real * real_twist + imag * imag_twist,
                    imag * real_twist - real * imag_twist,
                ],
                axis=0,
            )
        )
    columns = []
    for first in range(0, count, 2):
        high, low = halves(jnp.concatenate(turned[first : first + 2], axis=1))
        pair = mm(back_ref[...], jnp.concatenate([high, low, high], axis=0))
        columns += [pair[:, :LANES], pair[:, LANES:]]
    return columns


def spectrum_kernel(filters_ref, wide_ref, twist_ref, mix_ref, out_ref):
    channels, outer, _ = filters_ref.shape
    norm = 1.0 / (outer * LANES)

    @pl.loop(0, channels // GROUP)
    def _(step):
        columns = [filters_ref[step * GROUP + k] * norm for k in range(GROUP)]
        rows = spread(columns, wide_ref, twist_ref, False)
        span = GROUP * outer
        out_ref[pl.ds(pl.multiple_of(step * span, span), span), :] = mm_wide(rows, mix_ref)


def convolve(values_ref, spectrum_ref, tables, sign):
    exact_ref, twist_ref, mix_ref, unmix_ref, back_ref = tables
    outer = twist_ref.shape[0]
    channels = values_ref.shape[0] // outer
    span = GROUP * outer

    @pl.loop(0, channels // GROUP)
    def _(step):
        base = step * GROUP
        columns = [
            values_ref[pl.ds(base + k, outer, stride=channels), :] for k in range(GROUP)
        ]
        bins = mm_wide(spread(columns, exact_ref, twist_ref, True), mix_ref)
        filt = spectrum_ref[pl.ds(pl.multiple_of(step * span, span), span), :]
        real, imag = bins[:, :LANES], bins[:, LANES:]
        filt_real, filt_imag = filt[:, :LANES], filt[:, LANES:]
        product = jnp.concatenate(
            [
                real * filt_real - sign * (imag * filt_imag),
                imag * filt_real + sign * (real * filt_imag),
            ],
            axis=1,
        )
        result = gather_back(mm_wide(product, unmix_ref), back_ref, twist_ref)
        for k in range(GROUP):
            values_ref[pl.ds(base + k, outer, stride=channels), :] = result[k]


def one_hot_columns(ids, vocab):
    match = lax.broadcasted_iota(jnp.int32, (vocab, ids.shape[1]), 0) == ids
    return jnp.where(match, 1.0, 0.0).astype(BF16)


def swap_blocks(parts):
    lane = lax.broadcasted_iota(jnp.int32, parts[0].shape, 1) // SIDE
    out = []
    for to in range(HALVES):
        total = None
        for source in range(HALVES):
            moved = parts[source]
            if source != to:
                moved = pltpu.roll(moved, ((source - to) * SIDE) % LANES, 1)
            total = moved if total is None else jnp.where(lane == source, moved, total)
        out.append(total)
    return out


def send_kernel(ids_ref, ids_col_ref, embed_ref, weight_ref, grad_ref, inputs_ref, out_ref):
    tokens = ids_col_ref.shape[0]
    vocab, width = embed_ref.shape
    picks = lax.broadcasted_iota(jnp.int32, (tokens, vocab), 1) == ids_col_ref[...]
    picks = jnp.where(picks, 1.0, 0.0).astype(BF16)
    ids = ids_ref[...]
    high = ids // 2
    spare = lax.broadcasted_iota(jnp.int32, (8, tokens), 0)
    coded = jnp.where(spare == 0, high, jnp.where(spare == 1, ids - 2 * high, 0)).astype(F32)
    for block in range(width // LANES):
        lane = slice(block * LANES, (block + 1) * LANES)
        inputs = mm(picks, embed_ref[:, lane])
        inputs_ref[:, lane] = inputs.astype(BF16)
        upstream = grad_ref[:, lane].astype(F32) * inputs
        turned = upstream.T.astype(BF16)
        rows = [weight_ref[8 * g : 8 * g + 8, lane].astype(F32) for g in range(HALVES)]
        for k, piece in enumerate(swap_blocks(rows)):
            peer = block * HALVES + k
            out_ref[peer, 0:SIDE, :] = turned[k * SIDE : (k + 1) * SIDE]
            out_ref[peer, SIDE : SIDE + 16, :] = jnp.concatenate([piece, coded], axis=0).astype(
                BF16
            )


def read_ids(block_ref, peer):
    tail = block_ref[peer, SIDE : SIDE + 16, :].astype(F32)
    return (2.0 * tail[8:9] + tail[9:10]).astype(jnp.int32)


def forward_kernel(
    block_ref, embed_ref, spectrum_ref, exact_ref, twist_ref, mix_ref, unmix_ref, back_ref,
    out_ref, values_ref, weight_ref, table_ref,
):
    peers = block_ref.shape[0]
    vocab = embed_ref.shape[0]

    @pl.loop(0, peers)
    def _(peer):
        part = block_ref[peer, SIDE : SIDE + 16, :].astype(F32)[:8]
        lane = lax.broadcasted_iota(jnp.int32, part.shape, 1) // SIDE
        rows = [jnp.where(lane == g, part, 0.0) for g in range(HALVES)]
        weight_ref[pl.ds(pl.multiple_of(peer * SIDE, SIDE), SIDE), :] = jnp.concatenate(
            rows, axis=0
        ).astype(BF16)

    table = mm(embed_ref[...], weight_ref[...])
    table = table + pltpu.roll(table, 2 * SIDE, 1)
    table = table + pltpu.roll(table, SIDE, 1)
    table_ref[...] = table.T[:SIDE].astype(BF16)

    @pl.loop(0, peers // 2)
    def _(step):
        picks = [one_hot_columns(read_ids(block_ref, 2 * step + k), vocab) for k in range(2)]
        columns = mm(table_ref[...], jnp.concatenate(picks, axis=1)).astype(BF16).astype(F32)
        rows = jnp.concatenate([columns[:, :LANES], columns[:, LANES:]], axis=0)
        values_ref[pl.ds(pl.multiple_of(step * 2 * SIDE, 2 * SIDE), 2 * SIDE), :] = rows

    convolve(values_ref, spectrum_ref, (exact_ref, twist_ref, mix_ref, unmix_ref, back_ref), 1.0)
    out_ref[...] = values_ref[...].astype(BF16).reshape(out_ref.shape)


def backward_kernel(
    block_ref, embed_ref, spectrum_ref, exact_ref, twist_ref, mix_ref, unmix_ref, back_ref,
    out_ref, values_ref, sums_ref,
):
    peers = block_ref.shape[0]
    vocab, width = embed_ref.shape
    scaling = 1.0 / math.sqrt(peers * LANES)

    @pl.loop(0, peers)
    def _(peer):
        values_ref[pl.ds(pl.multiple_of(peer * SIDE, SIDE), SIDE), :] = block_ref[
            peer, 0:SIDE, :
        ].astype(F32)

    convolve(values_ref, spectrum_ref, (exact_ref, twist_ref, mix_ref, unmix_ref, back_ref), -1.0)
    sums_ref[...] = jnp.zeros_like(sums_ref)

    @pl.loop(0, peers // 2)
    def _(step):
        picks = [one_hot_columns(read_ids(block_ref, 2 * step + k), vocab) for k in range(2)]
        rows = values_ref[pl.ds(pl.multiple_of(step * 2 * SIDE, 2 * SIDE), 2 * SIDE), :]
        columns = jnp.concatenate([rows[:SIDE], rows[SIDE:]], axis=1).astype(BF16)
        sums_ref[...] += lax.dot_general(
            columns,
            jnp.concatenate(picks, axis=1),
            (((1,), (1,)), ((), ())),
            preferred_element_type=F32,
        )

    both = jnp.concatenate(halves(sums_ref[...]), axis=0)
    for block in range(width // LANES):
        lane = slice(block * LANES, (block + 1) * LANES)
        grad = mm(both, embed_ref[:, lane])
        grad = (grad[:SIDE] + grad[SIDE:]) * scaling
        shifted = [grad] + [pltpu.roll(grad, LANES - 8 * g, 1) for g in range(1, HALVES)]
        turned = jnp.concatenate(shifted, axis=0).T
        for k in range(HALVES):
            out_ref[block * HALVES + k] = turned[k * SIDE : k * SIDE + 8]


def momentum_kernel(grad_ref, momentum_ref, feedback_ref, updated_ref, residue_ref, quant_ref):
    width = momentum_ref.shape[1]
    for block in range(width // LANES):
        lane = slice(block * LANES, (block + 1) * LANES)
        parts = swap_blocks([grad_ref[block * HALVES + k] for k in range(HALVES)])
        grad = jnp.concatenate(parts, axis=0)
        updated_ref[:, lane] = momentum_keep * momentum_ref[:, lane] + (1.0 - momentum_keep) * grad
    total = updated_ref[...] + feedback_ref[...]
    scale = jnp.mean(jnp.abs(total), axis=1, keepdims=True) + tiny_shift
    quantized = (scale * jnp.clip(total / scale, -1.0, 1.0)).astype(BF16)
    quant_ref[...] = quantized
    residue_ref[...] = total - quantized.astype(F32)


def output_kernel(conv_ref, inputs_ref, out_ref):
    for block in range(out_ref.shape[1] // LANES):
        lane = slice(block * LANES, (block + 1) * LANES)
        rows = [conv_ref[block * HALVES + k].astype(F32) for k in range(HALVES)]
        conv = jnp.concatenate(rows, axis=0).T
        out_ref[:, lane] = (inputs_ref[:, lane].astype(F32) * conv).astype(BF16)


def call(kernel, out_shape, scratch=(), flops=0, moved=0):
    return pl.pallas_call(
        kernel,
        out_shape=out_shape,
        scratch_shapes=list(scratch),
        compiler_params=pltpu.CompilerParams(vmem_limit_bytes=VMEM_LIMIT),
        cost_estimate=pl.CostEstimate(flops=flops, bytes_accessed=moved, transcendentals=0),
    )


def exchange(values):
    return lax.all_to_all(values, "seq", split_axis=0, concat_axis=0, tiled=True)


def per_device(ids, embed, weight, filters, out_grad, momentum, feedback):
    parts = lax.axis_size("seq")
    replicas = lax.axis_size("dp")
    vocab, width = embed.shape
    tokens = ids.shape[1]
    channels = filters.shape[0]
    rows = channels * parts
    shape = jax.ShapeDtypeStruct
    tables = transform_tables(parts, tokens)
    convolve_tables = [tables[name] for name in ("exact", "twist", "mix", "unmix", "back")]

    inputs, block = call(
        send_kernel,
        (shape((tokens, width), BF16), shape((parts, SIDE + 16, tokens), BF16)),
        flops=2 * tokens * vocab * width,
        moved=5 << 20,
    )(ids, ids.reshape(tokens, 1), embed, weight, out_grad[0])
    block = exchange(block)
    spectrum = call(
        spectrum_kernel,
        shape((rows, 2 * tokens), F32),
        flops=5 << 30,
        moved=3 << 20,
    )(filters.reshape(channels, parts, tokens), tables["wide"], tables["twist"], tables["mix"])
    gradient = call(
        backward_kernel,
        shape((parts, 8, tokens), F32),
        [pltpu.VMEM((rows, tokens), F32), pltpu.VMEM((channels, vocab), F32)],
        flops=10 << 30,
        moved=6 << 20,
    )(block, embed, spectrum, *convolve_tables)
    gradient = exchange(gradient)
    convolved = call(
        forward_kernel,
        shape((parts, channels, tokens), BF16),
        [
            pltpu.VMEM((rows, tokens), F32),
            pltpu.VMEM((width, LANES), BF16),
            pltpu.VMEM((channels, vocab), BF16),
        ],
        flops=10 << 30,
        moved=6 << 20,
    )(block, embed, spectrum, *convolve_tables)
    convolved = exchange(convolved)
    updated, residue, quantized = call(
        momentum_kernel,
        (
            shape((weight.shape[0], width), F32),
            shape((weight.shape[0], width), F32),
            shape((weight.shape[0], width), BF16),
        ),
        flops=1 << 20,
        moved=2 << 20,
    )(gradient, momentum[0], feedback[0])
    sums = [quantized.astype(F32)]
    for flip in range(1, replicas):
        moved = lax.ppermute(
            quantized, "dp", [(source, source ^ flip) for source in range(replicas)]
        )
        sums.append(moved.astype(F32))
    while len(sums) > 1:
        sums = [left + right for left, right in zip(sums[0::2], sums[1::2])]
    summed = sums[0]
    new_weight = (weight.astype(F32) - step_rate * (summed / replicas)).astype(BF16)
    output = call(
        output_kernel, shape((tokens, width), BF16), flops=1 << 20, moved=2 << 20
    )(convolved, inputs)
    return (output[None], updated[None], residue[None], new_weight)


def solution(mesh):
    placed = (
        P("dp", "seq"),
        P(),
        P("seq", None),
        P("seq", None),
        P("dp", "seq", None),
        P("dp", "seq", None),
        P("dp", "seq", None),
    )
    return jax.shard_map(
        per_device,
        mesh=mesh,
        in_specs=placed,
        out_specs=(
            P("dp", "seq", None),
            P("dp", "seq", None),
            P("dp", "seq", None),
            P("seq", None),
        ),
        check_vma=False,
    )
```

```python
import functools
import math

import jax
import jax.numpy as jnp
import numpy as np
from jax import lax
from jax.experimental import pallas as pl
from jax.experimental.pallas import tpu as pltpu
from jax.sharding import PartitionSpec as P

momentum_keep = 0.9
step_rate = 0.02
tiny_shift = 1e-06

F32 = jnp.float32
BF16 = jnp.bfloat16
LANES = 128
GROUP = 16
STEP = 8
TAIL = 8
SENT = 6
HALVES = 4
SIDE = 32
VMEM_LIMIT = 58 * 1024 * 1024
CHUNKS = 2
TABLES = 4


def split_const(table):
    high = np.asarray(table, np.float32).astype(BF16)
    low = (table - high.astype(np.float64)).astype(np.float32).astype(BF16)
    return high, low


def transform_tables(outer, inner):
    total = outer * inner
    freq = np.arange(outer)[:, None] + 0.25
    first = np.exp(-2j * np.pi * freq * np.arange(outer)[None, :] / outer)
    twist = np.exp(-2j * np.pi * freq * np.arange(inner)[None, :] / total)
    second = np.exp(
        -2j * np.pi * (np.arange(inner)[:, None] * np.arange(inner)[None, :] % inner) / inner
    )
    stage = np.concatenate([first.real, first.imag], axis=0)
    high, low = split_const(stage)
    back_high, back_low = split_const(stage.T)
    real, imag = second.real, second.imag
    mix = np.block([[real, imag], [-imag, real]])
    return {
        "exact": np.concatenate([high, low], axis=1),
        "wide": np.concatenate([high, high, low], axis=1),
        "back": np.concatenate([back_high, back_high, back_low], axis=1),
        "twist": np.concatenate([twist.real, twist.imag], axis=1).astype(np.float32),
        "mix": np.stack(split_const(mix)),
    }


def mm(left, right):
    return jnp.dot(left, right, preferred_element_type=F32)


def halves(values):
    high = values.astype(BF16)
    return high, (values - high.astype(F32)).astype(BF16)


def mm_wide(values, table_ref):
    rows = values.shape[0]
    high, low = halves(values)
    both = mm(jnp.concatenate([high, low], axis=0), table_ref[0])
    return both[:rows] + both[rows:] + mm(high, table_ref[1])


def spread(columns, stage_ref, twist_ref, exact):
    real_twist = twist_ref[:, :LANES]
    imag_twist = twist_ref[:, LANES:]
    outer = real_twist.shape[0]
    rows = []
    for first in range(0, len(columns), 2):
        pair = jnp.concatenate(columns[first : first + 2], axis=1)
        if exact:
            high = pair.astype(BF16)
            stack = jnp.concatenate([high, high], axis=0)
        else:
            high, low = halves(pair)
            stack = jnp.concatenate([high, low, high], axis=0)
        grid = mm(stage_ref[...], stack)
        for which in range(2):
            lane = slice(which * LANES, (which + 1) * LANES)
            real = grid[:outer, lane]
            imag = grid[outer:, lane]
            rows.append(
                jnp.concatenate(
                    [
                        real * real_twist - imag * imag_twist,
                        real * imag_twist + imag * real_twist,
                    ],
                    axis=1,
                )
            )
    return jnp.concatenate(rows, axis=0)


def gather_back(spectrum, back_ref, twist_ref):
    real_twist = twist_ref[:, :LANES]
    imag_twist = twist_ref[:, LANES:]
    outer = real_twist.shape[0]
    count = spectrum.shape[0] // outer
    turned = []
    for which in range(count):
        real = spectrum[which * outer : (which + 1) * outer, :LANES]
        imag = spectrum[which * outer : (which + 1) * outer, LANES:]
        turned.append(
            jnp.concatenate(
                [
                    real * real_twist - imag * imag_twist,
                    -(imag * real_twist + real * imag_twist),
                ],
                axis=0,
            )
        )
    columns = []
    for first in range(0, count, 2):
        high, low = halves(jnp.concatenate(turned[first : first + 2], axis=1))
        pair = mm(back_ref[...], jnp.concatenate([high, low, high], axis=0))
        columns += [pair[:, :LANES], pair[:, LANES:]]
    return columns


def start_all(pairs, sems, first=0):
    copies = [
        pltpu.make_async_copy(source, target, sems.at[first + which])
        for which, (source, target) in enumerate(pairs)
    ]
    for copy in copies:
        copy.start()
    return copies


def wait_all(copies):
    for copy in copies:
        copy.wait()


def group_rows(which, outer):
    return pl.ds(which * GROUP * outer, GROUP * outer)


def token_picks(ids, vocab):
    column = jnp.broadcast_to(ids.astype(F32), (LANES, ids.shape[1])).T
    lane_index = lax.broadcasted_iota(jnp.int32, column.shape, 1).astype(F32)
    return jnp.concatenate(
        [
            jnp.where(column == lane_index + first, 1.0, 0.0).astype(BF16)
            for first in range(0, vocab, LANES)
        ],
        axis=1,
    )


def spectrum_kernel(
    filters_ref, wide_ref, twist_ref, mix_ref, ids_ref, embed_ref,
    out_hbm, inputs_ref, values_ref, out_ref, sems,
):
    channels, length = filters_ref.shape
    outer = length // LANES
    norm = 1.0 / length
    for block in range(outer):
        values_ref[block * channels : (block + 1) * channels, :] = (
            filters_ref[:, block * LANES : (block + 1) * LANES] * norm
        )
    copies = []
    for which in range(channels // GROUP):
        columns = [
            values_ref[pl.ds(which * GROUP + k, outer, stride=channels), :] for k in range(GROUP)
        ]
        bins = group_rows(which, outer)
        out_ref[bins, :] = mm_wide(spread(columns, wide_ref, twist_ref, False), mix_ref)
        copies += start_all([(out_ref.at[bins], out_hbm.at[bins])], sems, which)
    inputs_ref[...] = mm(token_picks(ids_ref[...], embed_ref.shape[0]), embed_ref[...]).astype(
        BF16
    )
    wait_all(copies)


def convolve(values_ref, spectrum_ref, tables, sign, arrivals):
    exact_ref, twist_ref, mix_ref, back_ref = tables
    outer = twist_ref.shape[0]
    channels = values_ref.shape[0] // outer
    for which in range(channels // GROUP):
        base = which * GROUP
        columns = [
            values_ref[pl.ds(base + k, outer, stride=channels), :] for k in range(GROUP)
        ]
        bins = mm_wide(spread(columns, exact_ref, twist_ref, True), mix_ref)
        arrivals[which].wait()
        filt = spectrum_ref[group_rows(which, outer), :]
        real, imag = bins[:, :LANES], bins[:, LANES:]
        filt_real, filt_imag = filt[:, :LANES], filt[:, LANES:]
        product = jnp.concatenate(
            [
                real * filt_real - sign * (imag * filt_imag),
                -(imag * filt_real + sign * (real * filt_imag)),
            ],
            axis=1,
        )
        result = gather_back(mm_wide(product, mix_ref), back_ref, twist_ref)
        for k in range(GROUP):
            values_ref[pl.ds(base + k, outer, stride=channels), :] = result[k]


def swap_blocks(parts):
    lane = lax.broadcasted_iota(jnp.int32, parts[0].shape, 1) // SIDE
    out = []
    for to in range(HALVES):
        total = None
        for source in range(HALVES):
            moved = parts[source]
            if source != to:
                moved = pltpu.roll(moved, ((source - to) * SIDE) % LANES, 1)
            total = moved if total is None else jnp.where(lane == source, moved, total)
        out.append(total)
    return out


def lane_span(chunk, width):
    span = width // CHUNKS
    return pl.ds(chunk * span, span)


def peer_span(chunk, peers):
    span = peers // CHUNKS
    return pl.ds(chunk * span, span)


def second_core():
    return lax.axis_index("dp") % 2 == 1


def send_kernel(
    ids_ref, embed_hbm, grad_hbm, weight_hbm, out_hbm,
    embed_ref, grad_ref, weight_ref, out_ref, sems,
):
    vocab, width = embed_hbm.shape
    tokens = ids_ref.shape[1]
    peers = out_ref.shape[0]
    copies = start_all([(weight_hbm, weight_ref), (grad_hbm, grad_ref)], sems, 2 * CHUNKS)
    for chunk in range(CHUNKS):
        lane = lane_span(chunk, width)
        copies += start_all([(embed_hbm.at[:, lane], embed_ref.at[:, lane])], sems, chunk)
    ids = ids_ref[...]
    high = ids // LANES
    spare = lax.broadcasted_iota(jnp.int32, (TAIL - SENT, tokens), 0)
    coded = jnp.where(spare == 0, high, ids - LANES * high).astype(F32)
    picks = token_picks(ids, vocab)
    late = second_core()
    sent = []
    wait_all(copies[:2])
    for chunk in range(CHUNKS):
        copies[2 + chunk].wait()
        blocks = width // LANES // CHUNKS
        for block in range(chunk * blocks, (chunk + 1) * blocks):
            lane = slice(block * LANES, (block + 1) * LANES)
            inputs = mm(picks, embed_ref[:, lane]).astype(BF16).astype(F32)
            turned = (grad_ref[:, lane].astype(F32) * inputs).T
            part = weight_ref[:, lane].astype(F32)
            parts = swap_blocks([part[8 * g : 8 * g + 8] for g in range(HALVES)])
            for k, piece in enumerate(parts):
                rows = [
                    turned[k * SIDE : (k + 1) * SIDE],
                    piece[:4],
                    jnp.where(late, piece[6:8], piece[4:6]),
                    coded,
                ]
                out_ref[block * HALVES + k] = jnp.concatenate(rows, axis=0).astype(BF16)
        rows = peer_span(chunk, peers)
        sent += start_all([(out_ref.at[rows], out_hbm.at[rows])], sems, CHUNKS + chunk)
    wait_all(sent)


def read_ids(block_ref, first):
    tails = [block_ref[first + k].astype(F32)[SIDE + SENT :] for k in range(2)]
    both = jnp.concatenate(tails, axis=1)
    high, low = both[0:1], both[1:2]
    index = lax.broadcasted_iota(jnp.int32, (LANES, 2 * LANES), 0).astype(F32)
    return high, jnp.where(index == low, 1.0, 0.0).astype(BF16)


def forward_kernel(
    block_hbm, other_hbm, embed_hbm, spectrum_hbm, exact_hbm, twist_hbm, mix_hbm, back_hbm,
    out_hbm,
    block_ref, other_ref, embed_ref, spectrum_ref, exact_ref, twist_ref, mix_ref, back_ref,
    values_ref, weight_ref, table_ref, out_ref, sems,
):
    peers = block_ref.shape[0]
    vocab, width = embed_ref.shape
    groups = SIDE // GROUP
    half = width // 2
    block_copy, other_copy, embed_first, embed_second = start_all(
        [
            (block_hbm, block_ref),
            (other_hbm, other_ref),
            (embed_hbm.at[:, pl.ds(0, half)], embed_ref.at[:, pl.ds(0, half)]),
            (embed_hbm.at[:, pl.ds(half, half)], embed_ref.at[:, pl.ds(half, half)]),
        ],
        sems,
    )
    table_copies = start_all(
        [
            (exact_hbm, exact_ref),
            (twist_hbm, twist_ref),
            (mix_hbm, mix_ref),
            (back_hbm, back_ref),
        ],
        sems,
        4,
    )
    spectrum_copies = start_all(
        [
            (spectrum_hbm.at[group_rows(k, peers)], spectrum_ref.at[group_rows(k, peers)])
            for k in range(groups)
        ],
        sems,
        4 + TABLES,
    )
    block_copy.wait()
    other_copy.wait()
    late = second_core()

    @pl.loop(0, peers // STEP)
    def _(step):
        others = other_ref[pl.ds(pl.multiple_of(step * 2 * STEP, 2 * STEP), 2 * STEP), :]
        others = others.astype(F32)
        for k in range(STEP):
            peer = step * STEP + k
            tail = block_ref[peer].astype(F32)[SIDE : SIDE + SENT]
            mine, other = tail[4:], others[2 * k : 2 * k + 2]
            part = jnp.concatenate(
                [tail[:4], jnp.where(late, other, mine), jnp.where(late, mine, other)], axis=0
            )
            lane = lax.broadcasted_iota(jnp.int32, part.shape, 1) // SIDE
            rows = [jnp.where(lane == g, part, 0.0) for g in range(HALVES)]
            weight_ref[pl.ds(pl.multiple_of(peer * SIDE, SIDE), SIDE), :] = jnp.concatenate(
                rows, axis=0
            ).astype(BF16)

    embed_first.wait()
    table = mm(embed_ref[:, :half], weight_ref[:half])
    embed_second.wait()
    table = table + mm(embed_ref[:, half:], weight_ref[half:])
    table = table + pltpu.roll(table, 2 * SIDE, 1)
    table = table + pltpu.roll(table, SIDE, 1)
    parts = []
    for part in range(vocab // LANES):
        turned = table[part * LANES : (part + 1) * LANES].T
        parts.append(turned[:SIDE])
    table_ref[...] = jnp.concatenate(parts, axis=0).astype(BF16)

    @pl.loop(0, peers // STEP)
    def _(step):
        for k in range(0, STEP, 2):
            first = step * STEP + k
            high, picks = read_ids(block_ref, first)
            every = mm(table_ref[...], picks)
            columns = every[:SIDE]
            for part in range(1, vocab // LANES):
                columns = jnp.where(
                    high == part, every[part * SIDE : (part + 1) * SIDE], columns
                )
            rows = jnp.concatenate([columns[:, :LANES], columns[:, LANES:]], axis=0)
            values_ref[pl.ds(pl.multiple_of(first * SIDE, 2 * SIDE), 2 * SIDE), :] = rows

    wait_all(table_copies)
    convolve(
        values_ref, spectrum_ref, (exact_ref, twist_ref, mix_ref, back_ref), 1.0, spectrum_copies
    )
    span = peers // CHUNKS
    copies = []
    for chunk in range(CHUNKS):
        rows = pl.ds(chunk * span, span)
        out_ref[rows] = (
            values_ref[pl.ds(chunk * span * SIDE, span * SIDE), :]
            .astype(BF16)
            .reshape(span, SIDE, LANES)
        )
        copies += start_all([(out_ref.at[rows], out_hbm.at[rows])], sems, 4 + TABLES + groups + chunk)
    wait_all(copies)


def backward_kernel(
    block_hbm, embed_hbm, spectrum_hbm, exact_hbm, twist_hbm, mix_hbm, back_hbm,
    out_hbm, other_hbm,
    block_ref, embed_ref, spectrum_ref, exact_ref, twist_ref, mix_ref, back_ref,
    values_ref, sums_ref, out_ref, other_ref, sems,
):
    peers = block_ref.shape[0]
    vocab, width = embed_ref.shape
    groups = SIDE // GROUP
    scaling = 1.0 / math.sqrt(peers * LANES)
    block_copies = start_all(
        [
            (block_hbm, block_ref),
            (exact_hbm, exact_ref),
            (twist_hbm, twist_ref),
            (mix_hbm, mix_ref),
            (back_hbm, back_ref),
        ],
        sems,
    )
    block_copies[0].wait()
    spectrum_copies = start_all(
        [
            (spectrum_hbm.at[group_rows(k, peers)], spectrum_ref.at[group_rows(k, peers)])
            for k in range(groups)
        ],
        sems,
        1 + TABLES,
    )
    (embed_copy,) = start_all([(embed_hbm, embed_ref)], sems, 1 + TABLES + groups)

    @pl.loop(0, peers // STEP)
    def _(step):
        others = []
        for k in range(STEP):
            peer = step * STEP + k
            part = block_ref[peer].astype(F32)
            values_ref[pl.ds(pl.multiple_of(peer * SIDE, SIDE), SIDE), :] = part[:SIDE]
            others.append(part[SIDE + 4 : SIDE + SENT])
        other_ref[pl.ds(pl.multiple_of(step * 2 * STEP, 2 * STEP), 2 * STEP), :] = (
            jnp.concatenate(others, axis=0).astype(BF16)
        )

    copies = start_all([(other_ref, other_hbm)], sems, 2 + TABLES + groups)
    wait_all(block_copies[1:])
    convolve(
        values_ref, spectrum_ref, (exact_ref, twist_ref, mix_ref, back_ref), -1.0, spectrum_copies
    )
    sums_ref[...] = jnp.zeros_like(sums_ref)

    @pl.loop(0, peers // STEP)
    def _(step):
        total = sums_ref[...]
        for k in range(0, STEP, 2):
            first = step * STEP + k
            high, picks = read_ids(block_ref, first)
            rows = values_ref[pl.ds(pl.multiple_of(first * SIDE, 2 * SIDE), 2 * SIDE), :]
            columns = jnp.concatenate([rows[:SIDE], rows[SIDE:]], axis=1)
            masked = [jnp.where(high == part, columns, 0.0) for part in range(vocab // LANES)]
            total = total + lax.dot_general(
                jnp.concatenate(masked, axis=0).astype(BF16),
                picks,
                (((1,), (1,)), ((), ())),
                preferred_element_type=F32,
            )
        sums_ref[...] = total

    sums = sums_ref[...]
    sums = jnp.concatenate(
        [sums[part * SIDE : (part + 1) * SIDE] for part in range(vocab // LANES)], axis=1
    )
    both = jnp.concatenate(halves(sums), axis=0)
    embed_copy.wait()
    blocks = width // LANES // CHUNKS
    for chunk in range(CHUNKS):
        for first in range(chunk * blocks, (chunk + 1) * blocks, 2):
            pair = mm(both, embed_ref[:, first * LANES : (first + 2) * LANES])
            pair = (pair[:SIDE] + pair[SIDE:]) * scaling
            for block in range(first, first + 2):
                lane = slice((block - first) * LANES, (block - first + 1) * LANES)
                grad = pair[:, lane]
                shifted = [grad] + [pltpu.roll(grad, LANES - 8 * g, 1) for g in range(1, HALVES)]
                turned = jnp.concatenate(shifted, axis=0).T
                for k in range(HALVES):
                    out_ref[block * HALVES + k] = turned[k * SIDE : k * SIDE + 8]
        rows = pl.ds(chunk * blocks * HALVES, blocks * HALVES)
        copies += start_all([(out_ref.at[rows], out_hbm.at[rows])], sems, 3 + TABLES + groups + chunk)
    wait_all(copies)


def momentum_kernel(
    grad_hbm, momentum_hbm, feedback_hbm, updated_hbm, residue_hbm, quant_hbm,
    grad_ref, updated_ref, total_ref, quant_ref, sems,
):
    peers = grad_ref.shape[0]
    width = total_ref.shape[1]
    blocks = width // LANES // CHUNKS
    copies = []
    for chunk in range(CHUNKS):
        lane = lane_span(chunk, width)
        rows = peer_span(chunk, peers)
        pairs = [
            (grad_hbm.at[rows], grad_ref.at[rows]),
            (momentum_hbm.at[:, lane], updated_ref.at[:, lane]),
            (feedback_hbm.at[:, lane], total_ref.at[:, lane]),
        ]
        copies.append(start_all(pairs, sems, 3 * chunk))
    sent = []
    weight = 0.0
    for chunk in range(CHUNKS):
        wait_all(copies[chunk])
        for block in range(chunk * blocks, (chunk + 1) * blocks):
            lane = slice(block * LANES, (block + 1) * LANES)
            parts = swap_blocks([grad_ref[block * HALVES + k] for k in range(HALVES)])
            grad = jnp.concatenate(parts, axis=0)
            updated = momentum_keep * updated_ref[:, lane] + (1.0 - momentum_keep) * grad
            updated_ref[:, lane] = updated
            total = updated + total_ref[:, lane]
            total_ref[:, lane] = total
            weight = weight + jnp.abs(total)
        lane = lane_span(chunk, width)
        sent += start_all(
            [(updated_ref.at[:, lane], updated_hbm.at[:, lane])], sems, 3 * CHUNKS + chunk
        )
    scale = jnp.sum(weight, axis=1, keepdims=True) / width + tiny_shift
    for chunk in range(CHUNKS):
        for block in range(chunk * blocks, (chunk + 1) * blocks):
            lane = slice(block * LANES, (block + 1) * LANES)
            total = total_ref[:, lane]
            quantized = (scale * jnp.clip(total / scale, -1.0, 1.0)).astype(BF16)
            quant_ref[:, lane] = quantized
            total_ref[:, lane] = total - quantized.astype(F32)
        lane = lane_span(chunk, width)
        pairs = [
            (quant_ref.at[:, lane], quant_hbm.at[:, lane]),
            (total_ref.at[:, lane], residue_hbm.at[:, lane]),
        ]
        sent += start_all(pairs, sems, 4 * CHUNKS + 2 * chunk)
    wait_all(sent)


def output_kernel(conv_hbm, inputs_hbm, out_hbm, conv_ref, inputs_ref, out_ref, sems):
    peers = conv_ref.shape[0]
    width = out_ref.shape[1]
    blocks = width // LANES // CHUNKS
    copies = []
    for chunk in range(CHUNKS):
        lane = lane_span(chunk, width)
        rows = peer_span(chunk, peers)
        pairs = [
            (conv_hbm.at[rows], conv_ref.at[rows]),
            (inputs_hbm.at[:, lane], inputs_ref.at[:, lane]),
        ]
        copies.append(start_all(pairs, sems, 2 * chunk))
    sent = []
    for chunk in range(CHUNKS):
        wait_all(copies[chunk])
        for block in range(chunk * blocks, (chunk + 1) * blocks):
            lane = slice(block * LANES, (block + 1) * LANES)
            rows = [conv_ref[block * HALVES + k].astype(F32) for k in range(HALVES)]
            conv = jnp.concatenate(rows, axis=0).T
            out_ref[:, lane] = (inputs_ref[:, lane].astype(F32) * conv).astype(BF16)
        lane = lane_span(chunk, width)
        sent += start_all([(out_ref.at[:, lane], out_hbm.at[:, lane])], sems, 2 * CHUNKS + chunk)
    wait_all(sent)


def spaces(kinds):
    return [
        pl.BlockSpec(memory_space={"h": pltpu.HBM, "a": pl.ANY, "v": pltpu.VMEM}[kind])
        for kind in kinds
    ]


def call(kernel, out_shape, ins, outs, scratch=(), flops=0, moved=0):
    out_specs = spaces(outs)
    return pl.pallas_call(
        kernel,
        out_shape=out_shape,
        in_specs=spaces(ins),
        out_specs=out_specs if len(outs) > 1 else out_specs[0],
        scratch_shapes=list(scratch),
        compiler_params=pltpu.CompilerParams(vmem_limit_bytes=VMEM_LIMIT),
        cost_estimate=pl.CostEstimate(flops=flops, bytes_accessed=moved, transcendentals=0),
    )


def exchange(values):
    return lax.all_to_all(values, "seq", split_axis=0, concat_axis=0, tiled=True)


def per_device(ids, embed, weight, filters, out_grad, momentum, feedback):
    parts = lax.axis_size("seq")
    replicas = lax.axis_size("dp")
    vocab, width = embed.shape
    tokens = ids.shape[1]
    channels = filters.shape[0]
    rows = channels * parts
    shape = jax.ShapeDtypeStruct
    tables = transform_tables(parts, tokens)
    convolve_tables = [tables[name] for name in ("exact", "twist", "mix", "back")]

    table_scratch = [
        pltpu.VMEM(table.shape, F32 if table.dtype == np.float32 else BF16)
        for table in convolve_tables
    ]
    groups = channels // GROUP

    block = call(
        send_kernel,
        shape((parts, SIDE + TAIL, tokens), BF16),
        "vhhh",
        "h",
        [
            pltpu.VMEM((vocab, width), BF16),
            pltpu.VMEM((tokens, width), BF16),
            pltpu.VMEM((weight.shape[0], width), BF16),
            pltpu.VMEM((parts, SIDE + TAIL, tokens), BF16),
            pltpu.SemaphoreType.DMA((2 * CHUNKS + 2,)),
        ],
        flops=2 * tokens * vocab * width,
        moved=5 << 20,
    )(ids, embed, out_grad[0], weight)
    block = exchange(block)
    spectrum, inputs = call(
        spectrum_kernel,
        (shape((rows, 2 * tokens), F32), shape((tokens, width), BF16)),
        "vvvvvv",
        "hv",
        [
            pltpu.VMEM((rows, tokens), F32),
            pltpu.VMEM((rows, 2 * tokens), F32),
            pltpu.SemaphoreType.DMA((groups,)),
        ],
        flops=5 << 30,
        moved=3 << 20,
    )(filters, tables["wide"], tables["twist"], tables["mix"], ids, embed)
    gradient, other = call(
        backward_kernel,
        (shape((parts, 8, tokens), F32), shape((2 * parts, tokens), BF16)),
        "ahhhhhh",
        "hh",
        [
            pltpu.VMEM((parts, SIDE + TAIL, tokens), BF16),
            pltpu.VMEM((vocab, width), BF16),
            pltpu.VMEM((rows, 2 * tokens), F32),
            *table_scratch,
            pltpu.VMEM((rows, tokens), F32),
            pltpu.VMEM((LANES, LANES), F32),
            pltpu.VMEM((parts, 8, tokens), F32),
            pltpu.VMEM((2 * parts, tokens), BF16),
            pltpu.SemaphoreType.DMA((3 + TABLES + groups + CHUNKS,)),
        ],
        flops=10 << 30,
        moved=6 << 20,
    )(block, embed, spectrum, *convolve_tables)
    other = lax.ppermute(other, "dp", [(source, source ^ 1) for source in range(replicas)])
    gradient = exchange(gradient)
    convolved = call(
        forward_kernel,
        shape((parts, channels, tokens), BF16),
        "aahhhhhh",
        "h",
        [
            pltpu.VMEM((parts, SIDE + TAIL, tokens), BF16),
            pltpu.VMEM((2 * parts, tokens), BF16),
            pltpu.VMEM((vocab, width), BF16),
            pltpu.VMEM((rows, 2 * tokens), F32),
            *table_scratch,
            pltpu.VMEM((rows, tokens), F32),
            pltpu.VMEM((width, LANES), BF16),
            pltpu.VMEM((LANES, LANES), BF16),
            pltpu.VMEM((parts, channels, tokens), BF16),
            pltpu.SemaphoreType.DMA((4 + TABLES + groups + CHUNKS,)),
        ],
        flops=10 << 30,
        moved=6 << 20,
    )(block, other, embed, spectrum, *convolve_tables)
    convolved = exchange(convolved)
    updated, residue, quantized = call(
        momentum_kernel,
        (
            shape((weight.shape[0], width), F32),
            shape((weight.shape[0], width), F32),
            shape((weight.shape[0], width), BF16),
        ),
        "ahh",
        "hhh",
        [
            pltpu.VMEM((parts, 8, tokens), F32),
            pltpu.VMEM((weight.shape[0], width), F32),
            pltpu.VMEM((weight.shape[0], width), F32),
            pltpu.VMEM((weight.shape[0], width), BF16),
            pltpu.SemaphoreType.DMA((6 * CHUNKS,)),
        ],
        flops=1 << 20,
        moved=2 << 20,
    )(gradient, momentum[0], feedback[0])
    def swap(values, flip):
        return lax.ppermute(values, "dp", [(source, source ^ flip) for source in range(replicas)])

    across = swap(quantized, 2)
    beside = swap(quantized, 1)
    corner = swap(across, 1)
    summed = (quantized.astype(F32) + beside.astype(F32)) + (
        across.astype(F32) + corner.astype(F32)
    )
    new_weight = (weight.astype(F32) - step_rate * (summed / replicas)).astype(BF16)
    output = call(
        output_kernel,
        shape((tokens, width), BF16),
        "aa",
        "h",
        [
            pltpu.VMEM((parts, channels, tokens), BF16),
            pltpu.VMEM((tokens, width), BF16),
            pltpu.VMEM((tokens, width), BF16),
            pltpu.SemaphoreType.DMA((3 * CHUNKS,)),
        ],
        flops=1 << 20,
        moved=2 << 20,
    )(convolved, inputs)
    return (output[None], updated[None], residue[None], new_weight)


def solution(mesh):
    placed = (
        P("dp", "seq"),
        P(),
        P("seq", None),
        P("seq", None),
        P("dp", "seq", None),
        P("dp", "seq", None),
        P("dp", "seq", None),
    )
    return jax.shard_map(
        per_device,
        mesh=mesh,
        in_specs=placed,
        out_specs=(
            P("dp", "seq", None),
            P("dp", "seq", None),
            P("dp", "seq", None),
            P("seq", None),
        ),
        check_vma=False,
    )
```

```python
import functools
import math

import jax
import jax.numpy as jnp
import numpy as np
from jax import lax
from jax.experimental import pallas as pl
from jax.experimental.pallas import tpu as pltpu
from jax.sharding import PartitionSpec as P

momentum_keep = 0.9
step_rate = 0.02
tiny_shift = 1e-06

F32 = jnp.float32
BF16 = jnp.bfloat16
LANES = 128
GROUP = 32
STEP = 32
TAIL = 8
SENT = 6
HALVES = 4
SIDE = 32
CHUNKS = 2
TABLES = 4


def split_const(table):
    high = np.asarray(table, np.float32).astype(BF16)
    low = (table - high.astype(np.float64)).astype(np.float32).astype(BF16)
    return high, low


def transform_tables(outer, inner):
    total = outer * inner
    freq = np.arange(outer)[:, None] + 0.25
    first = np.exp(-2j * np.pi * freq * np.arange(outer)[None, :] / outer)
    twist = np.exp(-2j * np.pi * freq * np.arange(inner)[None, :] / total)
    second = np.exp(
        -2j * np.pi * (np.arange(inner)[:, None] * np.arange(inner)[None, :] % inner) / inner
    )
    stage = np.concatenate([first.real, first.imag], axis=0)
    high, low = split_const(stage)
    back_high, back_low = split_const(stage.T)
    real, imag = second.real, second.imag
    mix = np.block([[real, imag], [-imag, real]])
    return {
        "exact": np.concatenate([high, low], axis=1),
        "wide": np.concatenate([high, high, low], axis=1),
        "back": np.concatenate([back_high, back_high, back_low], axis=1),
        "twist": np.concatenate([twist.real, twist.imag], axis=1).astype(np.float32),
        "mix": np.stack(split_const(mix)),
    }


def mm(left, right):
    return jnp.dot(left, right, preferred_element_type=F32)


def halves(values):
    high = values.astype(BF16)
    return high, (values - high.astype(F32)).astype(BF16)


def mm_wide(values, table_ref):
    rows = values.shape[0]
    high, low = halves(values)
    both = mm(jnp.concatenate([high, low], axis=0), table_ref[0])
    return both[:rows] + both[rows:] + mm(high, table_ref[1])


def spread(columns, stage_ref, twist_ref, exact):
    real_twist = twist_ref[:, :LANES]
    imag_twist = twist_ref[:, LANES:]
    outer = real_twist.shape[0]
    rows = []
    for first in range(0, len(columns), 2):
        pair = jnp.concatenate(columns[first : first + 2], axis=1)
        if exact:
            high = pair.astype(BF16)
            stack = jnp.concatenate([high, high], axis=0)
        else:
            high, low = halves(pair)
            stack = jnp.concatenate([high, low, high], axis=0)
        grid = mm(stage_ref[...], stack)
        for which in range(2):
            lane = slice(which * LANES, (which + 1) * LANES)
            real = grid[:outer, lane]
            imag = grid[outer:, lane]
            rows.append(
                jnp.concatenate(
                    [
                        real * real_twist - imag * imag_twist,
                        real * imag_twist + imag * real_twist,
                    ],
                    axis=1,
                )
            )
    return jnp.concatenate(rows, axis=0)


def gather_back(spectrum, back_ref, twist_ref):
    real_twist = twist_ref[:, :LANES]
    imag_twist = twist_ref[:, LANES:]
    outer = real_twist.shape[0]
    count = spectrum.shape[0] // outer
    turned = []
    for which in range(count):
        real = spectrum[which * outer : (which + 1) * outer, :LANES]
        imag = spectrum[which * outer : (which + 1) * outer, LANES:]
        turned.append(
            jnp.concatenate(
                [
                    real * real_twist - imag * imag_twist,
                    -(imag * real_twist + real * imag_twist),
                ],
                axis=0,
            )
        )
    columns = []
    for first in range(0, count, 2):
        high, low = halves(jnp.concatenate(turned[first : first + 2], axis=1))
        pair = mm(back_ref[...], jnp.concatenate([high, low, high], axis=0))
        columns += [pair[:, :LANES], pair[:, LANES:]]
    return columns


def start_all(pairs, sems, first=0):
    copies = [
        pltpu.make_async_copy(source, target, sems.at[first + which])
        for which, (source, target) in enumerate(pairs)
    ]
    for copy in copies:
        copy.start()
    return copies


def wait_all(copies):
    for copy in copies:
        copy.wait()


def group_rows(which, outer):
    return pl.ds(which * GROUP * outer, GROUP * outer)


def token_picks(ids, vocab):
    column = jnp.broadcast_to(ids.astype(F32), (LANES, ids.shape[1])).T
    lane_index = lax.broadcasted_iota(jnp.int32, column.shape, 1).astype(F32)
    return jnp.concatenate(
        [
            jnp.where(column == lane_index + first, 1.0, 0.0).astype(BF16)
            for first in range(0, vocab, LANES)
        ],
        axis=1,
    )


def spectrum_kernel(
    filters_ref, wide_ref, twist_ref, mix_ref, ids_ref, embed_ref,
    out_hbm, inputs_ref, values_ref, out_ref, sems,
):
    channels, length = filters_ref.shape
    outer = length // LANES
    norm = 1.0 / length
    for block in range(outer):
        values_ref[block * channels : (block + 1) * channels, :] = (
            filters_ref[:, block * LANES : (block + 1) * LANES] * norm
        )
    copies = []
    for which in range(channels // GROUP):
        columns = [
            values_ref[pl.ds(which * GROUP + k, outer, stride=channels), :] for k in range(GROUP)
        ]
        bins = group_rows(which, outer)
        out_ref[bins, :] = mm_wide(spread(columns, wide_ref, twist_ref, False), mix_ref)
        copies += start_all([(out_ref.at[bins], out_hbm.at[bins])], sems, which)
    inputs_ref[...] = mm(token_picks(ids_ref[...], embed_ref.shape[0]), embed_ref[...]).astype(
        BF16
    )
    wait_all(copies)


def convolve(values_ref, spectrum_ref, tables, sign, arrivals):
    exact_ref, twist_ref, mix_ref, back_ref = tables
    outer = twist_ref.shape[0]
    channels = values_ref.shape[0] // outer
    for which in range(channels // GROUP):
        base = which * GROUP
        columns = [
            values_ref[pl.ds(base + k, outer, stride=channels), :] for k in range(GROUP)
        ]
        bins = mm_wide(spread(columns, exact_ref, twist_ref, True), mix_ref)
        arrivals[which].wait()
        filt = spectrum_ref[group_rows(which, outer), :]
        real, imag = bins[:, :LANES], bins[:, LANES:]
        filt_real, filt_imag = filt[:, :LANES], filt[:, LANES:]
        product = jnp.concatenate(
            [
                real * filt_real - sign * (imag * filt_imag),
                -(imag * filt_real + sign * (real * filt_imag)),
            ],
            axis=1,
        )
        result = gather_back(mm_wide(product, mix_ref), back_ref, twist_ref)
        for k in range(GROUP):
            values_ref[pl.ds(base + k, outer, stride=channels), :] = result[k]


def swap_blocks(parts):
    lane = lax.broadcasted_iota(jnp.int32, parts[0].shape, 1) // SIDE
    out = []
    for to in range(HALVES):
        total = None
        for source in range(HALVES):
            moved = parts[source]
            if source != to:
                moved = pltpu.roll(moved, ((source - to) * SIDE) % LANES, 1)
            total = moved if total is None else jnp.where(lane == source, moved, total)
        out.append(total)
    return out


def lane_span(chunk, width):
    span = width // CHUNKS
    return pl.ds(chunk * span, span)


def peer_span(chunk, peers):
    span = peers // CHUNKS
    return pl.ds(chunk * span, span)


def second_core():
    return lax.axis_index("dp") % 2 == 1


def send_kernel(
    ids_ref, embed_hbm, grad_hbm, weight_hbm, out_hbm,
    embed_ref, grad_ref, weight_ref, out_ref, sems,
):
    vocab, width = embed_hbm.shape
    tokens = ids_ref.shape[1]
    peers = out_ref.shape[0]
    copies = start_all([(weight_hbm, weight_ref), (grad_hbm, grad_ref)], sems, 2 * CHUNKS)
    for chunk in range(CHUNKS):
        lane = lane_span(chunk, width)
        copies += start_all([(embed_hbm.at[:, lane], embed_ref.at[:, lane])], sems, chunk)
    ids = ids_ref[...]
    high = ids // LANES
    spare = lax.broadcasted_iota(jnp.int32, (TAIL - SENT, tokens), 0)
    coded = jnp.where(spare == 0, high, ids - LANES * high).astype(F32)
    picks = token_picks(ids, vocab)
    late = second_core()
    sent = []
    wait_all(copies[:2])
    for chunk in range(CHUNKS):
        copies[2 + chunk].wait()
        blocks = width // LANES // CHUNKS
        for block in range(chunk * blocks, (chunk + 1) * blocks):
            lane = slice(block * LANES, (block + 1) * LANES)
            inputs = mm(picks, embed_ref[:, lane]).astype(BF16).astype(F32)
            turned = (grad_ref[:, lane].astype(F32) * inputs).T
            part = weight_ref[:, lane].astype(F32)
            parts = swap_blocks([part[8 * g : 8 * g + 8] for g in range(HALVES)])
            for k, piece in enumerate(parts):
                rows = [
                    turned[k * SIDE : (k + 1) * SIDE],
                    piece[:4],
                    jnp.where(late, piece[6:8], piece[4:6]),
                    coded,
                ]
                out_ref[block * HALVES + k] = jnp.concatenate(rows, axis=0).astype(BF16)
        rows = peer_span(chunk, peers)
        sent += start_all([(out_ref.at[rows], out_hbm.at[rows])], sems, CHUNKS + chunk)
    wait_all(sent)


def read_ids(tails_ref, first):
    start = pl.multiple_of(first * TAIL, 2 * TAIL)
    tails = tails_ref[pl.ds(start, 2 * TAIL), :].astype(F32)
    both = jnp.concatenate([tails[SENT:TAIL], tails[TAIL + SENT :]], axis=1)
    high, low = both[0:1], both[1:2]
    index = lax.broadcasted_iota(jnp.int32, (LANES, 2 * LANES), 0).astype(F32)
    return high, jnp.where(index == low, 1.0, 0.0).astype(BF16)


def forward_kernel(
    tails_hbm, other_hbm, embed_hbm, spectrum_hbm, exact_hbm, twist_hbm, mix_hbm, back_hbm,
    out_hbm,
    tails_ref, other_ref, embed_ref, spectrum_ref, exact_ref, twist_ref, mix_ref, back_ref,
    values_ref, weight_ref, table_ref, out_ref, sems,
):
    peers = tails_ref.shape[0] // TAIL
    vocab, width = embed_ref.shape
    groups = SIDE // GROUP
    half = width // 2
    tails_copy, other_copy, embed_first, embed_second = start_all(
        [
            (tails_hbm, tails_ref),
            (other_hbm, other_ref),
            (embed_hbm.at[:, pl.ds(0, half)], embed_ref.at[:, pl.ds(0, half)]),
            (embed_hbm.at[:, pl.ds(half, half)], embed_ref.at[:, pl.ds(half, half)]),
        ],
        sems,
    )
    table_copies = start_all(
        [
            (exact_hbm, exact_ref),
            (twist_hbm, twist_ref),
            (mix_hbm, mix_ref),
            (back_hbm, back_ref),
        ],
        sems,
        4,
    )
    spectrum_copies = start_all(
        [
            (spectrum_hbm.at[group_rows(k, peers)], spectrum_ref.at[group_rows(k, peers)])
            for k in range(groups)
        ],
        sems,
        4 + TABLES,
    )
    tails_copy.wait()
    other_copy.wait()
    late = second_core()

    @pl.loop(0, peers // STEP)
    def _(step):
        others = other_ref[pl.ds(pl.multiple_of(step * 2 * STEP, 2 * STEP), 2 * STEP), :]
        others = others.astype(F32)
        tails = tails_ref[pl.ds(pl.multiple_of(step * TAIL * STEP, TAIL * STEP), TAIL * STEP), :]
        tails = tails.astype(F32)
        for k in range(STEP):
            peer = step * STEP + k
            tail = tails[k * TAIL : (k + 1) * TAIL]
            mine, other = tail[4:SENT], others[2 * k : 2 * k + 2]
            part = jnp.concatenate(
                [tail[:4], jnp.where(late, other, mine), jnp.where(late, mine, other)], axis=0
            )
            lane = lax.broadcasted_iota(jnp.int32, part.shape, 1) // SIDE
            rows = [jnp.where(lane == g, part, 0.0) for g in range(HALVES)]
            weight_ref[pl.ds(pl.multiple_of(peer * SIDE, SIDE), SIDE), :] = jnp.concatenate(
                rows, axis=0
            ).astype(BF16)

    embed_first.wait()
    table = mm(embed_ref[:, :half], weight_ref[:half])
    embed_second.wait()
    table = table + mm(embed_ref[:, half:], weight_ref[half:])
    table = table + pltpu.roll(table, 2 * SIDE, 1)
    table = table + pltpu.roll(table, SIDE, 1)
    parts = []
    for part in range(vocab // LANES):
        turned = table[part * LANES : (part + 1) * LANES].T
        parts.append(turned[:SIDE])
    table_ref[...] = jnp.concatenate(parts, axis=0).astype(BF16)

    @pl.loop(0, peers // STEP)
    def _(step):
        for k in range(0, STEP, 2):
            first = step * STEP + k
            high, picks = read_ids(tails_ref, first)
            every = mm(table_ref[...], picks)
            columns = every[:SIDE]
            for part in range(1, vocab // LANES):
                columns = jnp.where(
                    high == part, every[part * SIDE : (part + 1) * SIDE], columns
                )
            rows = jnp.concatenate([columns[:, :LANES], columns[:, LANES:]], axis=0)
            values_ref[pl.ds(pl.multiple_of(first * SIDE, 2 * SIDE), 2 * SIDE), :] = rows

    wait_all(table_copies)
    convolve(
        values_ref, spectrum_ref, (exact_ref, twist_ref, mix_ref, back_ref), 1.0, spectrum_copies
    )
    span = peers // CHUNKS
    copies = []
    for chunk in range(CHUNKS):
        rows = pl.ds(chunk * span, span)
        out_ref[rows] = (
            values_ref[pl.ds(chunk * span * SIDE, span * SIDE), :]
            .astype(BF16)
            .reshape(span, SIDE, LANES)
        )
        copies += start_all([(out_ref.at[rows], out_hbm.at[rows])], sems, 4 + TABLES + groups + chunk)
    wait_all(copies)


def backward_kernel(
    block_ref, embed_hbm, spectrum_hbm, exact_hbm, twist_hbm, mix_hbm, back_hbm,
    out_hbm, other_hbm, tails_hbm,
    embed_ref, spectrum_ref, exact_ref, twist_ref, mix_ref, back_ref,
    values_ref, sums_ref, out_ref, other_ref, tails_ref, sems,
):
    peers = block_ref.shape[0]
    vocab, width = embed_ref.shape
    groups = SIDE // GROUP
    scaling = 1.0 / math.sqrt(peers * LANES)
    table_copies = start_all(
        [
            (exact_hbm, exact_ref),
            (twist_hbm, twist_ref),
            (mix_hbm, mix_ref),
            (back_hbm, back_ref),
        ],
        sems,
    )
    spectrum_copies = start_all(
        [
            (spectrum_hbm.at[group_rows(k, peers)], spectrum_ref.at[group_rows(k, peers)])
            for k in range(groups)
        ],
        sems,
        1 + TABLES,
    )
    (embed_copy,) = start_all([(embed_hbm, embed_ref)], sems, 1 + TABLES + groups)

    @pl.loop(0, peers // STEP)
    def _(step):
        others, tails = [], []
        for k in range(STEP):
            peer = step * STEP + k
            part = block_ref[peer].astype(F32)
            values_ref[pl.ds(pl.multiple_of(peer * SIDE, SIDE), SIDE), :] = part[:SIDE]
            others.append(part[SIDE + 4 : SIDE + SENT])
            tails.append(part[SIDE:])
        other_ref[pl.ds(pl.multiple_of(step * 2 * STEP, 2 * STEP), 2 * STEP), :] = (
            jnp.concatenate(others, axis=0).astype(BF16)
        )
        tails_ref[pl.ds(pl.multiple_of(step * TAIL * STEP, TAIL * STEP), TAIL * STEP), :] = (
            jnp.concatenate(tails, axis=0).astype(BF16)
        )

    copies = start_all(
        [(other_ref, other_hbm), (tails_ref, tails_hbm)], sems, 2 + TABLES + groups
    )
    wait_all(table_copies)
    convolve(
        values_ref, spectrum_ref, (exact_ref, twist_ref, mix_ref, back_ref), -1.0, spectrum_copies
    )
    sums_ref[...] = jnp.zeros_like(sums_ref)

    @pl.loop(0, peers // STEP)
    def _(step):
        total = sums_ref[...]
        for k in range(0, STEP, 2):
            first = step * STEP + k
            high, picks = read_ids(tails_ref, first)
            rows = values_ref[pl.ds(pl.multiple_of(first * SIDE, 2 * SIDE), 2 * SIDE), :]
            columns = jnp.concatenate([rows[:SIDE], rows[SIDE:]], axis=1)
            masked = [jnp.where(high == part, columns, 0.0) for part in range(vocab // LANES)]
            total = total + lax.dot_general(
                jnp.concatenate(masked, axis=0).astype(BF16),
                picks,
                (((1,), (1,)), ((), ())),
                preferred_element_type=F32,
            )
        sums_ref[...] = total

    sums = sums_ref[...]
    sums = jnp.concatenate(
        [sums[part * SIDE : (part + 1) * SIDE] for part in range(vocab // LANES)], axis=1
    )
    both = jnp.concatenate(halves(sums), axis=0)
    embed_copy.wait()
    blocks = width // LANES // CHUNKS
    for chunk in range(CHUNKS):
        for first in range(chunk * blocks, (chunk + 1) * blocks, 2):
            pair = mm(both, embed_ref[:, first * LANES : (first + 2) * LANES])
            pair = (pair[:SIDE] + pair[SIDE:]) * scaling
            for block in range(first, first + 2):
                lane = slice((block - first) * LANES, (block - first + 1) * LANES)
                grad = pair[:, lane]
                shifted = [grad] + [pltpu.roll(grad, LANES - 8 * g, 1) for g in range(1, HALVES)]
                turned = jnp.concatenate(shifted, axis=0).T
                for k in range(HALVES):
                    out_ref[block * HALVES + k] = turned[k * SIDE : k * SIDE + 8]
        rows = pl.ds(chunk * blocks * HALVES, blocks * HALVES)
        copies += start_all([(out_ref.at[rows], out_hbm.at[rows])], sems, 4 + TABLES + groups + chunk)
    wait_all(copies)


def momentum_kernel(
    grad_hbm, momentum_hbm, feedback_hbm, updated_hbm, residue_hbm, quant_hbm,
    grad_ref, updated_ref, total_ref, quant_ref, sems,
):
    peers = grad_ref.shape[0]
    width = total_ref.shape[1]
    blocks = width // LANES // CHUNKS
    copies = []
    for chunk in range(CHUNKS):
        lane = lane_span(chunk, width)
        rows = peer_span(chunk, peers)
        pairs = [
            (grad_hbm.at[rows], grad_ref.at[rows]),
            (momentum_hbm.at[:, lane], updated_ref.at[:, lane]),
            (feedback_hbm.at[:, lane], total_ref.at[:, lane]),
        ]
        copies.append(start_all(pairs, sems, 3 * chunk))
    sent = []
    weight = 0.0
    for chunk in range(CHUNKS):
        wait_all(copies[chunk])
        for block in range(chunk * blocks, (chunk + 1) * blocks):
            lane = slice(block * LANES, (block + 1) * LANES)
            parts = swap_blocks([grad_ref[block * HALVES + k] for k in range(HALVES)])
            grad = jnp.concatenate(parts, axis=0)
            updated = momentum_keep * updated_ref[:, lane] + (1.0 - momentum_keep) * grad
            updated_ref[:, lane] = updated
            total = updated + total_ref[:, lane]
            total_ref[:, lane] = total
            weight = weight + jnp.abs(total)
        lane = lane_span(chunk, width)
        sent += start_all(
            [(updated_ref.at[:, lane], updated_hbm.at[:, lane])], sems, 3 * CHUNKS + chunk
        )
    scale = jnp.sum(weight, axis=1, keepdims=True) / width + tiny_shift
    for chunk in range(CHUNKS):
        for block in range(chunk * blocks, (chunk + 1) * blocks):
            lane = slice(block * LANES, (block + 1) * LANES)
            total = total_ref[:, lane]
            quantized = (scale * jnp.clip(total / scale, -1.0, 1.0)).astype(BF16)
            quant_ref[:, lane] = quantized
            total_ref[:, lane] = total - quantized.astype(F32)
        lane = lane_span(chunk, width)
        pairs = [
            (quant_ref.at[:, lane], quant_hbm.at[:, lane]),
            (total_ref.at[:, lane], residue_hbm.at[:, lane]),
        ]
        sent += start_all(pairs, sems, 4 * CHUNKS + 2 * chunk)
    wait_all(sent)


def output_kernel(conv_ref, inputs_hbm, out_hbm, inputs_ref, out_ref, sems):
    width = out_ref.shape[1]
    blocks = width // LANES // CHUNKS
    copies = []
    for chunk in range(CHUNKS):
        lane = lane_span(chunk, width)
        copies += start_all([(inputs_hbm.at[:, lane], inputs_ref.at[:, lane])], sems, chunk)
    sent = []
    for chunk in range(CHUNKS):
        copies[chunk].wait()
        for block in range(chunk * blocks, (chunk + 1) * blocks):
            lane = slice(block * LANES, (block + 1) * LANES)
            rows = [conv_ref[block * HALVES + k].astype(F32) for k in range(HALVES)]
            conv = jnp.concatenate(rows, axis=0).T
            out_ref[:, lane] = (inputs_ref[:, lane].astype(F32) * conv).astype(BF16)
        lane = lane_span(chunk, width)
        sent += start_all([(out_ref.at[:, lane], out_hbm.at[:, lane])], sems, CHUNKS + chunk)
    wait_all(sent)


def spaces(kinds):
    return [
        pl.BlockSpec(memory_space={"h": pltpu.HBM, "a": pl.ANY, "v": pltpu.VMEM}[kind])
        for kind in kinds
    ]


def call(kernel, out_shape, ins, outs, scratch=(), flops=0, moved=0, limit=60817408):
    out_specs = spaces(outs)
    return pl.pallas_call(
        kernel,
        out_shape=out_shape,
        in_specs=spaces(ins),
        out_specs=out_specs if len(outs) > 1 else out_specs[0],
        scratch_shapes=list(scratch),
        compiler_params=pltpu.CompilerParams(vmem_limit_bytes=limit),
        cost_estimate=pl.CostEstimate(flops=flops, bytes_accessed=moved, transcendentals=0),
    )


def exchange(values):
    return lax.all_to_all(values, "seq", split_axis=0, concat_axis=0, tiled=True)


def per_device(ids, embed, weight, filters, out_grad, momentum, feedback):
    parts = lax.axis_size("seq")
    replicas = lax.axis_size("dp")
    vocab, width = embed.shape
    tokens = ids.shape[1]
    channels = filters.shape[0]
    rows = channels * parts
    shape = jax.ShapeDtypeStruct
    tables = transform_tables(parts, tokens)
    convolve_tables = [tables[name] for name in ("exact", "twist", "mix", "back")]

    table_scratch = [
        pltpu.VMEM(table.shape, F32 if table.dtype == np.float32 else BF16)
        for table in convolve_tables
    ]
    groups = channels // GROUP

    block = call(
        send_kernel,
        shape((parts, SIDE + TAIL, tokens), BF16),
        "vhhh",
        "h",
        [
            pltpu.VMEM((vocab, width), BF16),
            pltpu.VMEM((tokens, width), BF16),
            pltpu.VMEM((weight.shape[0], width), BF16),
            pltpu.VMEM((parts, SIDE + TAIL, tokens), BF16),
            pltpu.SemaphoreType.DMA((2 * CHUNKS + 2,)),
        ],
        flops=2 * tokens * vocab * width,
        moved=5 << 20,
    )(ids, embed, out_grad[0], weight)
    block = exchange(block)
    spectrum, inputs = call(
        spectrum_kernel,
        (shape((rows, 2 * tokens), F32), shape((tokens, width), BF16)),
        "vvvvvv",
        "hv",
        [
            pltpu.VMEM((rows, tokens), F32),
            pltpu.VMEM((rows, 2 * tokens), F32),
            pltpu.SemaphoreType.DMA((groups,)),
        ],
        flops=5 << 30,
        moved=3 << 20,
        limit=16777216,
    )(filters, tables["wide"], tables["twist"], tables["mix"], ids, embed)
    gradient, other, tails = call(
        backward_kernel,
        (
            shape((parts, 8, tokens), F32),
            shape((2 * parts, tokens), BF16),
            shape((TAIL * parts, tokens), BF16),
        ),
        "vhhhhhh",
        "hhh",
        [
            pltpu.VMEM((vocab, width), BF16),
            pltpu.VMEM((rows, 2 * tokens), F32),
            *table_scratch,
            pltpu.VMEM((rows, tokens), F32),
            pltpu.VMEM((LANES, LANES), F32),
            pltpu.VMEM((parts, 8, tokens), F32),
            pltpu.VMEM((2 * parts, tokens), BF16),
            pltpu.VMEM((TAIL * parts, tokens), BF16),
            pltpu.SemaphoreType.DMA((4 + TABLES + groups + CHUNKS,)),
        ],
        flops=10 << 30,
        moved=6 << 20,
        limit=62820000,
    )(block, embed, spectrum, *convolve_tables)
    other = lax.ppermute(other, "dp", [(source, source ^ 1) for source in range(replicas)])
    gradient = exchange(gradient)
    convolved = call(
        forward_kernel,
        shape((parts, channels, tokens), BF16),
        "aahhhhhh",
        "h",
        [
            pltpu.VMEM((TAIL * parts, tokens), BF16),
            pltpu.VMEM((2 * parts, tokens), BF16),
            pltpu.VMEM((vocab, width), BF16),
            pltpu.VMEM((rows, 2 * tokens), F32),
            *table_scratch,
            pltpu.VMEM((rows, tokens), F32),
            pltpu.VMEM((width, LANES), BF16),
            pltpu.VMEM((LANES, LANES), BF16),
            pltpu.VMEM((parts, channels, tokens), BF16),
            pltpu.SemaphoreType.DMA((4 + TABLES + groups + CHUNKS,)),
        ],
        flops=10 << 30,
        moved=6 << 20,
        limit=60817408,
    )(tails, other, embed, spectrum, *convolve_tables)
    convolved = exchange(convolved)
    updated, residue, quantized = call(
        momentum_kernel,
        (
            shape((weight.shape[0], width), F32),
            shape((weight.shape[0], width), F32),
            shape((weight.shape[0], width), BF16),
        ),
        "ahh",
        "hhh",
        [
            pltpu.VMEM((parts, 8, tokens), F32),
            pltpu.VMEM((weight.shape[0], width), F32),
            pltpu.VMEM((weight.shape[0], width), F32),
            pltpu.VMEM((weight.shape[0], width), BF16),
            pltpu.SemaphoreType.DMA((6 * CHUNKS,)),
        ],
        flops=1 << 20,
        moved=2 << 20,
        limit=60817408,
    )(gradient, momentum[0], feedback[0])
    def swap(values, flip):
        return lax.ppermute(values, "dp", [(source, source ^ flip) for source in range(replicas)])

    across = swap(quantized, 2)
    beside = swap(quantized, 1)
    corner = swap(across, 1)
    summed = (quantized.astype(F32) + beside.astype(F32)) + (
        across.astype(F32) + corner.astype(F32)
    )
    new_weight = (weight.astype(F32) - step_rate * (summed / replicas)).astype(BF16)
    output = call(
        output_kernel,
        shape((tokens, width), BF16),
        "va",
        "h",
        [
            pltpu.VMEM((tokens, width), BF16),
            pltpu.VMEM((tokens, width), BF16),
            pltpu.SemaphoreType.DMA((2 * CHUNKS,)),
        ],
        flops=1 << 20,
        moved=2 << 20,
        limit=16777216,
    )(convolved, inputs)
    return (output[None], updated[None], residue[None], new_weight)


def solution(mesh):
    placed = (
        P("dp", "seq"),
        P(),
        P("seq", None),
        P("seq", None),
        P("dp", "seq", None),
        P("dp", "seq", None),
        P("dp", "seq", None),
    )
    return jax.shard_map(
        per_device,
        mesh=mesh,
        in_specs=placed,
        out_specs=(
            P("dp", "seq", None),
            P("dp", "seq", None),
            P("dp", "seq", None),
            P("seq", None),
        ),
        check_vma=False,
    )
```

```python
import functools
import math

import jax
import jax.numpy as jnp
import numpy as np
from jax import lax
from jax.experimental import pallas as pl
from jax.experimental.pallas import tpu as pltpu
from jax.sharding import PartitionSpec as P

momentum_keep = 0.9
step_rate = 0.02
tiny_shift = 1e-06

F32 = jnp.float32
BF16 = jnp.bfloat16
LANES = 128
GROUP = 32
STEP = 32
TAIL = 8
SENT = 6
HALVES = 4
SIDE = 32
CHUNKS = 2
TABLES = 4


def split_const(table):
    high = np.asarray(table, np.float32).astype(BF16)
    low = (table - high.astype(np.float64)).astype(np.float32).astype(BF16)
    return high, low


def packed_mix(table):
    high, low = split_const(
        np.block([[table.real, table.imag], [-table.imag, table.real]])
    )
    return np.block([[high, low], [high, np.zeros_like(low)]])


def transform_tables(outer, inner):
    total = outer * inner
    freq = np.arange(outer)[:, None] + 0.25
    first = np.exp(-2j * np.pi * freq * np.arange(outer)[None, :] / outer)
    twist = np.exp(-2j * np.pi * freq * np.arange(inner)[None, :] / total)
    half = inner // 2
    near, bins = np.arange(half)[:, None], 2 * np.arange(half)[None, :]
    even = np.exp(-2j * np.pi * (near * bins % inner) / inner)
    odd = np.exp(-2j * np.pi * (near * (bins + 1) % inner) / inner)
    stage = np.concatenate([first.real, first.imag], axis=0)
    high, low = split_const(stage)
    back_high, back_low = split_const(stage.T)
    mixes = [packed_mix(table) for table in (even, odd, even.conj().T, odd.conj().T)]
    return {
        "exact": np.concatenate([high, low], axis=1),
        "wide": np.concatenate([high, high, low], axis=1),
        "back": np.concatenate([back_high, back_high, back_low], axis=1),
        "twist": np.concatenate([twist.real, twist.imag], axis=1).astype(np.float32),
        "mix": np.stack(mixes),
    }


def mm(left, right):
    return jnp.dot(left, right, preferred_element_type=F32)


def halves(values):
    high = values.astype(BF16)
    return high, (values - high.astype(F32)).astype(BF16)


def mm_packed(values, table):
    both = mm(jnp.concatenate(halves(values), axis=1), table)
    return both[:, :LANES] + both[:, LANES:]


def turn(values):
    return pltpu.roll(values, LANES // 2, 1)


def in_low(values):
    return lax.broadcasted_iota(jnp.int32, values.shape, 1) < LANES // 2


def spread(columns, stage_ref, twist_ref, exact):
    real_twist = twist_ref[:, :LANES]
    imag_twist = twist_ref[:, LANES:]
    outer = real_twist.shape[0]
    evens, odds = [], []
    for first in range(0, len(columns), 2):
        pair = jnp.concatenate(columns[first : first + 2], axis=1)
        if exact:
            high = pair.astype(BF16)
            stack = jnp.concatenate([high, high], axis=0)
        else:
            high, low = halves(pair)
            stack = jnp.concatenate([high, low, high], axis=0)
        grid = mm(stage_ref[...], stack)
        for which in range(2):
            lane = slice(which * LANES, (which + 1) * LANES)
            real = grid[:outer, lane]
            imag = grid[outer:, lane]
            spun_real = real * real_twist - imag * imag_twist
            spun_imag = real * imag_twist + imag * real_twist
            far_real, far_imag = turn(spun_real), turn(spun_imag)
            low = in_low(spun_real)
            evens.append(jnp.where(low, spun_real + far_real, spun_imag + far_imag))
            odds.append(jnp.where(low, spun_real - far_real, far_imag - spun_imag))
    return jnp.concatenate(evens, axis=0), jnp.concatenate(odds, axis=0)


def gather_back(even, odd, back_ref, twist_ref):
    real_twist = twist_ref[:, :LANES]
    imag_twist = twist_ref[:, LANES:]
    outer = real_twist.shape[0]
    count = even.shape[0] // outer
    turned = []
    for which in range(count):
        rows = slice(which * outer, (which + 1) * outer)
        total, change = even[rows] + odd[rows], even[rows] - odd[rows]
        low = in_low(total)
        real = jnp.where(low, total, turn(change))
        imag = jnp.where(low, turn(total), change)
        turned.append(
            jnp.concatenate(
                [
                    real * real_twist + imag * imag_twist,
                    imag * real_twist - real * imag_twist,
                ],
                axis=0,
            )
        )
    columns = []
    for first in range(0, count, 2):
        high, low = halves(jnp.concatenate(turned[first : first + 2], axis=1))
        pair = mm(back_ref[...], jnp.concatenate([high, low, high], axis=0))
        columns += [pair[:, :LANES], pair[:, LANES:]]
    return columns


def start_all(pairs, sems, first=0):
    copies = [
        pltpu.make_async_copy(source, target, sems.at[first + which])
        for which, (source, target) in enumerate(pairs)
    ]
    for copy in copies:
        copy.start()
    return copies


def wait_all(copies):
    for copy in copies:
        copy.wait()


def group_rows(which, outer):
    return pl.ds(which * GROUP * outer, GROUP * outer)


def token_picks(ids, vocab):
    column = jnp.broadcast_to(ids.astype(F32), (LANES, ids.shape[1])).T
    lane_index = lax.broadcasted_iota(jnp.int32, column.shape, 1).astype(F32)
    return jnp.concatenate(
        [
            jnp.where(column == lane_index + first, 1.0, 0.0).astype(BF16)
            for first in range(0, vocab, LANES)
        ],
        axis=1,
    )


def spectrum_kernel(
    filters_ref, wide_ref, twist_ref, mix_ref, ids_ref, embed_ref,
    out_hbm, inputs_ref, values_ref, out_ref, sems,
):
    channels, length = filters_ref.shape
    outer = length // LANES
    norm = 1.0 / length
    for block in range(outer):
        values_ref[block * channels : (block + 1) * channels, :] = (
            filters_ref[:, block * LANES : (block + 1) * LANES] * norm
        )
    copies = []
    for which in range(channels // GROUP):
        columns = [
            values_ref[pl.ds(which * GROUP + k, outer, stride=channels), :] for k in range(GROUP)
        ]
        bins = group_rows(which, outer)
        even, odd = spread(columns, wide_ref, twist_ref, False)
        out_ref[bins, :LANES] = mm_packed(even, mix_ref[0])
        out_ref[bins, LANES:] = mm_packed(odd, mix_ref[1])
        copies += start_all([(out_ref.at[bins], out_hbm.at[bins])], sems, which)
    inputs_ref[...] = mm(token_picks(ids_ref[...], embed_ref.shape[0]), embed_ref[...]).astype(
        BF16
    )
    wait_all(copies)


def convolve(values_ref, spectrum_ref, tables, sign, arrivals):
    exact_ref, twist_ref, mix_ref, back_ref = tables
    outer = twist_ref.shape[0]
    channels = values_ref.shape[0] // outer
    for which in range(channels // GROUP):
        base = which * GROUP
        columns = [
            values_ref[pl.ds(base + k, outer, stride=channels), :] for k in range(GROUP)
        ]
        pieces = spread(columns, exact_ref, twist_ref, True)
        bins = [mm_packed(piece, mix_ref[half]) for half, piece in enumerate(pieces)]
        arrivals[which].wait()
        filt = spectrum_ref[group_rows(which, outer), :]
        pieces = []
        for half in range(2):
            own = filt[:, half * LANES : (half + 1) * LANES]
            far = turn(own)
            low = in_low(own)
            straight = jnp.where(low, own, far)
            crossed = jnp.where(low, -sign * far, sign * own)
            product = bins[half] * straight + turn(bins[half]) * crossed
            pieces.append(mm_packed(product, mix_ref[2 + half]))
        result = gather_back(*pieces, back_ref, twist_ref)
        for k in range(GROUP):
            values_ref[pl.ds(base + k, outer, stride=channels), :] = result[k]


def swap_blocks(parts):
    lane = lax.broadcasted_iota(jnp.int32, parts[0].shape, 1) // SIDE
    out = []
    for to in range(HALVES):
        total = None
        for source in range(HALVES):
            moved = parts[source]
            if source != to:
                moved = pltpu.roll(moved, ((source - to) * SIDE) % LANES, 1)
            total = moved if total is None else jnp.where(lane == source, moved, total)
        out.append(total)
    return out


def lane_span(chunk, width):
    span = width // CHUNKS
    return pl.ds(chunk * span, span)


def peer_span(chunk, peers):
    span = peers // CHUNKS
    return pl.ds(chunk * span, span)


def second_core():
    return lax.axis_index("dp") % 2 == 1


def send_kernel(
    ids_ref, embed_hbm, grad_hbm, weight_hbm, out_hbm,
    embed_ref, grad_ref, weight_ref, out_ref, sems,
):
    vocab, width = embed_hbm.shape
    tokens = ids_ref.shape[1]
    peers = out_ref.shape[0]
    copies = start_all([(weight_hbm, weight_ref), (grad_hbm, grad_ref)], sems, 2 * CHUNKS)
    for chunk in range(CHUNKS):
        lane = lane_span(chunk, width)
        copies += start_all([(embed_hbm.at[:, lane], embed_ref.at[:, lane])], sems, chunk)
    ids = ids_ref[...]
    high = ids // LANES
    spare = lax.broadcasted_iota(jnp.int32, (TAIL - SENT, tokens), 0)
    coded = jnp.where(spare == 0, high, ids - LANES * high).astype(F32)
    picks = token_picks(ids, vocab)
    late = second_core()
    sent = []
    wait_all(copies[:2])
    for chunk in range(CHUNKS):
        copies[2 + chunk].wait()
        blocks = width // LANES // CHUNKS
        for block in range(chunk * blocks, (chunk + 1) * blocks):
            lane = slice(block * LANES, (block + 1) * LANES)
            if block % 2 == 0:
                pair = slice(block * LANES, (block + 2) * LANES)
                upstream = grad_ref[:, pair].astype(F32) * mm(picks, embed_ref[:, pair])
            turned = upstream[:, (block % 2) * LANES : (block % 2 + 1) * LANES].T
            part = weight_ref[:, lane].astype(F32)
            parts = swap_blocks([part[8 * g : 8 * g + 8] for g in range(HALVES)])
            for k, piece in enumerate(parts):
                rows = [
                    turned[k * SIDE : (k + 1) * SIDE],
                    piece[:4],
                    jnp.where(late, piece[6:8], piece[4:6]),
                    coded,
                ]
                out_ref[block * HALVES + k] = jnp.concatenate(rows, axis=0).astype(BF16)
        rows = peer_span(chunk, peers)
        sent += start_all([(out_ref.at[rows], out_hbm.at[rows])], sems, CHUNKS + chunk)
    wait_all(sent)


def read_ids(tails_ref, first):
    start = pl.multiple_of(first * TAIL, 2 * TAIL)
    tails = tails_ref[pl.ds(start, 2 * TAIL), :].astype(F32)
    both = jnp.concatenate([tails[SENT:TAIL], tails[TAIL + SENT :]], axis=1)
    high, low = both[0:1], both[1:2]
    index = lax.broadcasted_iota(jnp.int32, (LANES, 2 * LANES), 0).astype(F32)
    return high, jnp.where(index == low, 1.0, 0.0).astype(BF16)


def forward_kernel(
    tails_hbm, other_hbm, embed_hbm, spectrum_hbm, exact_hbm, twist_hbm, mix_hbm, back_hbm,
    out_hbm,
    tails_ref, other_ref, embed_ref, spectrum_ref, exact_ref, twist_ref, mix_ref, back_ref,
    values_ref, weight_ref, table_ref, out_ref, sems,
):
    peers = tails_ref.shape[0] // TAIL
    vocab, width = embed_ref.shape
    groups = SIDE // GROUP
    half = width // 2
    tails_copy, other_copy, embed_first, embed_second = start_all(
        [
            (tails_hbm, tails_ref),
            (other_hbm, other_ref),
            (embed_hbm.at[:, pl.ds(0, half)], embed_ref.at[:, pl.ds(0, half)]),
            (embed_hbm.at[:, pl.ds(half, half)], embed_ref.at[:, pl.ds(half, half)]),
        ],
        sems,
    )
    table_copies = start_all(
        [
            (exact_hbm, exact_ref),
            (twist_hbm, twist_ref),
            (mix_hbm, mix_ref),
            (back_hbm, back_ref),
        ],
        sems,
        4,
    )
    spectrum_copies = start_all(
        [
            (spectrum_hbm.at[group_rows(k, peers)], spectrum_ref.at[group_rows(k, peers)])
            for k in range(groups)
        ],
        sems,
        4 + TABLES,
    )
    tails_copy.wait()
    other_copy.wait()
    late = second_core()

    @pl.loop(0, peers // STEP)
    def _(step):
        others = other_ref[pl.ds(pl.multiple_of(step * 2 * STEP, 2 * STEP), 2 * STEP), :]
        others = others.astype(F32)
        tails = tails_ref[pl.ds(pl.multiple_of(step * TAIL * STEP, TAIL * STEP), TAIL * STEP), :]
        tails = tails.astype(F32)
        for k in range(STEP):
            peer = step * STEP + k
            tail = tails[k * TAIL : (k + 1) * TAIL]
            mine, other = tail[4:SENT], others[2 * k : 2 * k + 2]
            part = jnp.concatenate(
                [tail[:4], jnp.where(late, other, mine), jnp.where(late, mine, other)], axis=0
            )
            lane = lax.broadcasted_iota(jnp.int32, part.shape, 1) // SIDE
            rows = [jnp.where(lane == g, part, 0.0) for g in range(HALVES)]
            weight_ref[pl.ds(pl.multiple_of(peer * SIDE, SIDE), SIDE), :] = jnp.concatenate(
                rows, axis=0
            ).astype(BF16)

    embed_first.wait()
    table = mm(embed_ref[:, :half], weight_ref[:half])
    embed_second.wait()
    table = table + mm(embed_ref[:, half:], weight_ref[half:])
    table = table + pltpu.roll(table, 2 * SIDE, 1)
    table = table + pltpu.roll(table, SIDE, 1)
    parts = []
    for part in range(vocab // LANES):
        turned = table[part * LANES : (part + 1) * LANES].T
        parts.append(turned[:SIDE])
    table_ref[...] = jnp.concatenate(parts, axis=0).astype(BF16)

    @pl.loop(0, peers // STEP)
    def _(step):
        for k in range(0, STEP, 2):
            first = step * STEP + k
            high, picks = read_ids(tails_ref, first)
            every = mm(table_ref[...], picks)
            columns = every[:SIDE]
            for part in range(1, vocab // LANES):
                columns = jnp.where(
                    high == part, every[part * SIDE : (part + 1) * SIDE], columns
                )
            rows = jnp.concatenate([columns[:, :LANES], columns[:, LANES:]], axis=0)
            values_ref[pl.ds(pl.multiple_of(first * SIDE, 2 * SIDE), 2 * SIDE), :] = rows

    wait_all(table_copies)
    convolve(
        values_ref, spectrum_ref, (exact_ref, twist_ref, mix_ref, back_ref), 1.0, spectrum_copies
    )
    span = peers // CHUNKS
    copies = []
    for chunk in range(CHUNKS):
        rows = pl.ds(chunk * span, span)
        out_ref[rows] = (
            values_ref[pl.ds(chunk * span * SIDE, span * SIDE), :]
            .astype(BF16)
            .reshape(span, SIDE, LANES)
        )
        copies += start_all([(out_ref.at[rows], out_hbm.at[rows])], sems, 4 + TABLES + groups + chunk)
    wait_all(copies)


def backward_kernel(
    block_ref, embed_hbm, spectrum_hbm, exact_hbm, twist_hbm, mix_hbm, back_hbm,
    out_hbm, other_hbm, tails_hbm,
    embed_ref, spectrum_ref, exact_ref, twist_ref, mix_ref, back_ref,
    values_ref, sums_ref, out_ref, other_ref, tails_ref, sems,
):
    peers = block_ref.shape[0]
    vocab, width = embed_ref.shape
    groups = SIDE // GROUP
    scaling = 1.0 / math.sqrt(peers * LANES)
    table_copies = start_all(
        [
            (exact_hbm, exact_ref),
            (twist_hbm, twist_ref),
            (mix_hbm, mix_ref),
            (back_hbm, back_ref),
        ],
        sems,
    )
    spectrum_copies = start_all(
        [
            (spectrum_hbm.at[group_rows(k, peers)], spectrum_ref.at[group_rows(k, peers)])
            for k in range(groups)
        ],
        sems,
        1 + TABLES,
    )
    (embed_copy,) = start_all([(embed_hbm, embed_ref)], sems, 1 + TABLES + groups)

    @pl.loop(0, peers // STEP)
    def _(step):
        others, tails = [], []
        for k in range(STEP):
            peer = step * STEP + k
            part = block_ref[peer].astype(F32)
            values_ref[pl.ds(pl.multiple_of(peer * SIDE, SIDE), SIDE), :] = part[:SIDE]
            others.append(part[SIDE + 4 : SIDE + SENT])
            tails.append(part[SIDE:])
        other_ref[pl.ds(pl.multiple_of(step * 2 * STEP, 2 * STEP), 2 * STEP), :] = (
            jnp.concatenate(others, axis=0).astype(BF16)
        )
        tails_ref[pl.ds(pl.multiple_of(step * TAIL * STEP, TAIL * STEP), TAIL * STEP), :] = (
            jnp.concatenate(tails, axis=0).astype(BF16)
        )

    copies = start_all(
        [(other_ref, other_hbm), (tails_ref, tails_hbm)], sems, 2 + TABLES + groups
    )
    wait_all(table_copies)
    convolve(
        values_ref, spectrum_ref, (exact_ref, twist_ref, mix_ref, back_ref), -1.0, spectrum_copies
    )
    sums_ref[...] = jnp.zeros_like(sums_ref)

    @pl.loop(0, peers // STEP)
    def _(step):
        total = sums_ref[...]
        for k in range(0, STEP, 2):
            first = step * STEP + k
            high, picks = read_ids(tails_ref, first)
            rows = values_ref[pl.ds(pl.multiple_of(first * SIDE, 2 * SIDE), 2 * SIDE), :]
            columns = jnp.concatenate([rows[:SIDE], rows[SIDE:]], axis=1)
            masked = [jnp.where(high == part, columns, 0.0) for part in range(vocab // LANES)]
            total = total + lax.dot_general(
                jnp.concatenate(masked, axis=0).astype(BF16),
                picks,
                (((1,), (1,)), ((), ())),
                preferred_element_type=F32,
            )
        sums_ref[...] = total

    sums = sums_ref[...]
    sums = jnp.concatenate(
        [sums[part * SIDE : (part + 1) * SIDE] for part in range(vocab // LANES)], axis=1
    )
    both = jnp.concatenate(halves(sums), axis=0)
    embed_copy.wait()
    blocks = width // LANES // CHUNKS
    for chunk in range(CHUNKS):
        for first in range(chunk * blocks, (chunk + 1) * blocks, 2):
            pair = mm(both, embed_ref[:, first * LANES : (first + 2) * LANES])
            pair = (pair[:SIDE] + pair[SIDE:]) * scaling
            for block in range(first, first + 2):
                lane = slice((block - first) * LANES, (block - first + 1) * LANES)
                grad = pair[:, lane]
                shifted = [grad] + [pltpu.roll(grad, LANES - 8 * g, 1) for g in range(1, HALVES)]
                turned = jnp.concatenate(shifted, axis=0).T
                for k in range(HALVES):
                    out_ref[block * HALVES + k] = turned[k * SIDE : k * SIDE + 8]
        rows = pl.ds(chunk * blocks * HALVES, blocks * HALVES)
        copies += start_all([(out_ref.at[rows], out_hbm.at[rows])], sems, 4 + TABLES + groups + chunk)
    wait_all(copies)


def momentum_kernel(
    grad_hbm, momentum_hbm, feedback_hbm, updated_hbm, residue_hbm, quant_hbm,
    grad_ref, updated_ref, total_ref, quant_ref, sems,
):
    peers = grad_ref.shape[0]
    width = total_ref.shape[1]
    blocks = width // LANES // CHUNKS
    copies = []
    for chunk in range(CHUNKS):
        lane = lane_span(chunk, width)
        rows = peer_span(chunk, peers)
        pairs = [
            (grad_hbm.at[rows], grad_ref.at[rows]),
            (momentum_hbm.at[:, lane], updated_ref.at[:, lane]),
            (feedback_hbm.at[:, lane], total_ref.at[:, lane]),
        ]
        copies.append(start_all(pairs, sems, 3 * chunk))
    sent = []
    weight = 0.0
    for chunk in range(CHUNKS):
        wait_all(copies[chunk])
        for block in range(chunk * blocks, (chunk + 1) * blocks):
            lane = slice(block * LANES, (block + 1) * LANES)
            parts = swap_blocks([grad_ref[block * HALVES + k] for k in range(HALVES)])
            grad = jnp.concatenate(parts, axis=0)
            updated = momentum_keep * updated_ref[:, lane] + (1.0 - momentum_keep) * grad
            updated_ref[:, lane] = updated
            total = updated + total_ref[:, lane]
            total_ref[:, lane] = total
            weight = weight + jnp.abs(total)
        lane = lane_span(chunk, width)
        sent += start_all(
            [(updated_ref.at[:, lane], updated_hbm.at[:, lane])], sems, 3 * CHUNKS + chunk
        )
    scale = jnp.sum(weight, axis=1, keepdims=True) / width + tiny_shift
    for chunk in range(CHUNKS):
        for block in range(chunk * blocks, (chunk + 1) * blocks):
            lane = slice(block * LANES, (block + 1) * LANES)
            total = total_ref[:, lane]
            quantized = (scale * jnp.clip(total / scale, -1.0, 1.0)).astype(BF16)
            quant_ref[:, lane] = quantized
            total_ref[:, lane] = total - quantized.astype(F32)
        lane = lane_span(chunk, width)
        pairs = [
            (quant_ref.at[:, lane], quant_hbm.at[:, lane]),
            (total_ref.at[:, lane], residue_hbm.at[:, lane]),
        ]
        sent += start_all(pairs, sems, 4 * CHUNKS + 2 * chunk)
    wait_all(sent)


def output_kernel(conv_ref, inputs_hbm, out_hbm, inputs_ref, out_ref, sems):
    width = out_ref.shape[1]
    blocks = width // LANES // CHUNKS
    copies = []
    for chunk in range(CHUNKS):
        lane = lane_span(chunk, width)
        copies += start_all([(inputs_hbm.at[:, lane], inputs_ref.at[:, lane])], sems, chunk)
    sent = []
    for chunk in range(CHUNKS):
        copies[chunk].wait()
        for block in range(chunk * blocks, (chunk + 1) * blocks):
            lane = slice(block * LANES, (block + 1) * LANES)
            rows = [conv_ref[block * HALVES + k].astype(F32) for k in range(HALVES)]
            conv = jnp.concatenate(rows, axis=0).T
            out_ref[:, lane] = (inputs_ref[:, lane].astype(F32) * conv).astype(BF16)
        lane = lane_span(chunk, width)
        sent += start_all([(out_ref.at[:, lane], out_hbm.at[:, lane])], sems, CHUNKS + chunk)
    wait_all(sent)


def spaces(kinds):
    return [
        pl.BlockSpec(memory_space={"h": pltpu.HBM, "a": pl.ANY, "v": pltpu.VMEM}[kind])
        for kind in kinds
    ]


def call(kernel, out_shape, ins, outs, scratch=(), flops=0, moved=0, limit=60817408):
    out_specs = spaces(outs)
    return pl.pallas_call(
        kernel,
        out_shape=out_shape,
        in_specs=spaces(ins),
        out_specs=out_specs if len(outs) > 1 else out_specs[0],
        scratch_shapes=list(scratch),
        compiler_params=pltpu.CompilerParams(vmem_limit_bytes=limit),
        cost_estimate=pl.CostEstimate(flops=flops, bytes_accessed=moved, transcendentals=0),
    )


def exchange(values):
    return lax.all_to_all(values, "seq", split_axis=0, concat_axis=0, tiled=True)


def per_device(ids, embed, weight, filters, out_grad, momentum, feedback):
    parts = lax.axis_size("seq")
    replicas = lax.axis_size("dp")
    vocab, width = embed.shape
    tokens = ids.shape[1]
    channels = filters.shape[0]
    rows = channels * parts
    shape = jax.ShapeDtypeStruct
    tables = transform_tables(parts, tokens)
    convolve_tables = [tables[name] for name in ("exact", "twist", "mix", "back")]

    table_scratch = [
        pltpu.VMEM(table.shape, F32 if table.dtype == np.float32 else BF16)
        for table in convolve_tables
    ]
    groups = channels // GROUP

    block = call(
        send_kernel,
        shape((parts, SIDE + TAIL, tokens), BF16),
        "vhhh",
        "h",
        [
            pltpu.VMEM((vocab, width), BF16),
            pltpu.VMEM((tokens, width), BF16),
            pltpu.VMEM((weight.shape[0], width), BF16),
            pltpu.VMEM((parts, SIDE + TAIL, tokens), BF16),
            pltpu.SemaphoreType.DMA((2 * CHUNKS + 2,)),
        ],
        flops=2 * tokens * vocab * width,
        moved=5 << 20,
    )(ids, embed, out_grad[0], weight)
    block = exchange(block)
    spectrum, inputs = call(
        spectrum_kernel,
        (shape((rows, 2 * tokens), F32), shape((tokens, width), BF16)),
        "vvvvvv",
        "hv",
        [
            pltpu.VMEM((rows, tokens), F32),
            pltpu.VMEM((rows, 2 * tokens), F32),
            pltpu.SemaphoreType.DMA((groups,)),
        ],
        flops=5 << 30,
        moved=3 << 20,
        limit=16777216,
    )(filters, tables["wide"], tables["twist"], tables["mix"], ids, embed)
    gradient, other, tails = call(
        backward_kernel,
        (
            shape((parts, 8, tokens), F32),
            shape((2 * parts, tokens), BF16),
            shape((TAIL * parts, tokens), BF16),
        ),
        "vhhhhhh",
        "hhh",
        [
            pltpu.VMEM((vocab, width), BF16),
            pltpu.VMEM((rows, 2 * tokens), F32),
            *table_scratch,
            pltpu.VMEM((rows, tokens), F32),
            pltpu.VMEM((LANES, LANES), F32),
            pltpu.VMEM((parts, 8, tokens), F32),
            pltpu.VMEM((2 * parts, tokens), BF16),
            pltpu.VMEM((TAIL * parts, tokens), BF16),
            pltpu.SemaphoreType.DMA((4 + TABLES + groups + CHUNKS,)),
        ],
        flops=10 << 30,
        moved=6 << 20,
        limit=62820000,
    )(block, embed, spectrum, *convolve_tables)
    other = lax.ppermute(other, "dp", [(source, source ^ 1) for source in range(replicas)])
    gradient = exchange(gradient)
    convolved = call(
        forward_kernel,
        shape((parts, channels, tokens), BF16),
        "aahhhhhh",
        "h",
        [
            pltpu.VMEM((TAIL * parts, tokens), BF16),
            pltpu.VMEM((2 * parts, tokens), BF16),
            pltpu.VMEM((vocab, width), BF16),
            pltpu.VMEM((rows, 2 * tokens), F32),
            *table_scratch,
            pltpu.VMEM((rows, tokens), F32),
            pltpu.VMEM((width, LANES), BF16),
            pltpu.VMEM((LANES, LANES), BF16),
            pltpu.VMEM((parts, channels, tokens), BF16),
            pltpu.SemaphoreType.DMA((4 + TABLES + groups + CHUNKS,)),
        ],
        flops=10 << 30,
        moved=6 << 20,
        limit=60817408,
    )(tails, other, embed, spectrum, *convolve_tables)
    convolved = exchange(convolved)
    updated, residue, quantized = call(
        momentum_kernel,
        (
            shape((weight.shape[0], width), F32),
            shape((weight.shape[0], width), F32),
            shape((weight.shape[0], width), BF16),
        ),
        "ahh",
        "hhh",
        [
            pltpu.VMEM((parts, 8, tokens), F32),
            pltpu.VMEM((weight.shape[0], width), F32),
            pltpu.VMEM((weight.shape[0], width), F32),
            pltpu.VMEM((weight.shape[0], width), BF16),
            pltpu.SemaphoreType.DMA((6 * CHUNKS,)),
        ],
        flops=1 << 20,
        moved=2 << 20,
        limit=60817408,
    )(gradient, momentum[0], feedback[0])
    def swap(values, flip):
        return lax.ppermute(values, "dp", [(source, source ^ flip) for source in range(replicas)])

    across = swap(quantized, 2)
    beside = swap(quantized, 1)
    corner = swap(across, 1)
    summed = (quantized.astype(F32) + beside.astype(F32)) + (
        across.astype(F32) + corner.astype(F32)
    )
    new_weight = (weight.astype(F32) - step_rate * (summed / replicas)).astype(BF16)
    output = call(
        output_kernel,
        shape((tokens, width), BF16),
        "va",
        "h",
        [
            pltpu.VMEM((tokens, width), BF16),
            pltpu.VMEM((tokens, width), BF16),
            pltpu.SemaphoreType.DMA((2 * CHUNKS,)),
        ],
        flops=1 << 20,
        moved=2 << 20,
        limit=16777216,
    )(convolved, inputs)
    return (output[None], updated[None], residue[None], new_weight)


def solution(mesh):
    placed = (
        P("dp", "seq"),
        P(),
        P("seq", None),
        P("seq", None),
        P("dp", "seq", None),
        P("dp", "seq", None),
        P("dp", "seq", None),
    )
    return jax.shard_map(
        per_device,
        mesh=mesh,
        in_specs=placed,
        out_specs=(
            P("dp", "seq", None),
            P("dp", "seq", None),
            P("dp", "seq", None),
            P("seq", None),
        ),
        check_vma=False,
    )
```

```python
import functools
import math

import jax
import jax.numpy as jnp
import numpy as np
from jax import lax
from jax.experimental import pallas as pl
from jax.experimental.pallas import tpu as pltpu
from jax.sharding import PartitionSpec as P

momentum_keep = 0.9
step_rate = 0.02
tiny_shift = 1e-06

F32 = jnp.float32
BF16 = jnp.bfloat16
LANES = 128
GROUP = 16
STEP = 32
TAIL = 8
SENT = 6
HALVES = 4
SIDE = 32
CHUNKS = 2
TABLES = 4


def split_const(table):
    high = np.asarray(table, np.float32).astype(BF16)
    low = (table - high.astype(np.float64)).astype(np.float32).astype(BF16)
    return high, low


def packed_mix(table):
    high, low = split_const(
        np.block([[table.real, table.imag], [-table.imag, table.real]])
    )
    return np.block([[high, low], [high, np.zeros_like(low)]])


def transform_tables(outer, inner):
    total = outer * inner
    freq = np.arange(outer)[:, None] + 0.25
    first = np.exp(-2j * np.pi * freq * np.arange(outer)[None, :] / outer)
    twist = np.exp(-2j * np.pi * freq * np.arange(inner)[None, :] / total)
    half = inner // 2
    near, bins = np.arange(half)[:, None], 2 * np.arange(half)[None, :]
    even = np.exp(-2j * np.pi * (near * bins % inner) / inner)
    odd = np.exp(-2j * np.pi * (near * (bins + 1) % inner) / inner)
    stage = np.concatenate([first.real, first.imag], axis=0)
    high, low = split_const(stage)
    back_high, back_low = split_const(stage.T)
    mixes = [packed_mix(table) for table in (even, odd, even.conj().T, odd.conj().T)]
    return {
        "exact": np.concatenate([high, low], axis=1),
        "wide": np.concatenate([high, high, low], axis=1),
        "back": np.concatenate([back_high, back_high, back_low], axis=1),
        "twist": np.concatenate([twist.real, twist.imag], axis=1).astype(np.float32),
        "mix": np.stack(mixes),
    }


def mm(left, right):
    return jnp.dot(left, right, preferred_element_type=F32)


def halves(values):
    high = values.astype(BF16)
    return high, (values - high.astype(F32)).astype(BF16)


def mm_packed(values, table):
    both = mm(jnp.concatenate(halves(values), axis=1), table)
    return both[:, :LANES] + both[:, LANES:]


def turn(values):
    return pltpu.roll(values, LANES // 2, 1)


def in_low(values):
    return lax.broadcasted_iota(jnp.int32, values.shape, 1) < LANES // 2


def spread(columns, stage_ref, twist_ref, exact):
    real_twist = twist_ref[:, :LANES]
    imag_twist = twist_ref[:, LANES:]
    outer = real_twist.shape[0]
    evens, odds = [], []
    for first in range(0, len(columns), 2):
        pair = jnp.concatenate(columns[first : first + 2], axis=1)
        if exact:
            high = pair.astype(BF16)
            stack = jnp.concatenate([high, high], axis=0)
        else:
            high, low = halves(pair)
            stack = jnp.concatenate([high, low, high], axis=0)
        grid = mm(stage_ref[...], stack)
        for which in range(2):
            lane = slice(which * LANES, (which + 1) * LANES)
            real = grid[:outer, lane]
            imag = grid[outer:, lane]
            spun_real = real * real_twist - imag * imag_twist
            spun_imag = real * imag_twist + imag * real_twist
            far_real, far_imag = turn(spun_real), turn(spun_imag)
            low = in_low(spun_real)
            evens.append(jnp.where(low, spun_real + far_real, spun_imag + far_imag))
            odds.append(jnp.where(low, spun_real - far_real, far_imag - spun_imag))
    return jnp.concatenate(evens, axis=0), jnp.concatenate(odds, axis=0)


def gather_back(even, odd, back_ref, twist_ref):
    real_twist = twist_ref[:, :LANES]
    imag_twist = twist_ref[:, LANES:]
    outer = real_twist.shape[0]
    count = even.shape[0] // outer
    turned = []
    for which in range(count):
        rows = slice(which * outer, (which + 1) * outer)
        total, change = even[rows] + odd[rows], even[rows] - odd[rows]
        low = in_low(total)
        real = jnp.where(low, total, turn(change))
        imag = jnp.where(low, turn(total), change)
        turned.append(
            jnp.concatenate(
                [
                    real * real_twist + imag * imag_twist,
                    imag * real_twist - real * imag_twist,
                ],
                axis=0,
            )
        )
    columns = []
    for first in range(0, count, 2):
        high, low = halves(jnp.concatenate(turned[first : first + 2], axis=1))
        pair = mm(back_ref[...], jnp.concatenate([high, low, high], axis=0))
        columns += [pair[:, :LANES], pair[:, LANES:]]
    return columns


def start_all(pairs, sems, first=0):
    copies = [
        pltpu.make_async_copy(source, target, sems.at[first + which])
        for which, (source, target) in enumerate(pairs)
    ]
    for copy in copies:
        copy.start()
    return copies


def wait_all(copies):
    for copy in copies:
        copy.wait()


def group_rows(which, outer):
    return pl.ds(which * GROUP * outer, GROUP * outer)


def token_picks(ids, vocab):
    column = jnp.broadcast_to(ids.astype(F32), (LANES, ids.shape[1])).T
    lane_index = lax.broadcasted_iota(jnp.int32, column.shape, 1).astype(F32)
    return jnp.concatenate(
        [
            jnp.where(column == lane_index + first, 1.0, 0.0).astype(BF16)
            for first in range(0, vocab, LANES)
        ],
        axis=1,
    )


def spectrum_kernel(
    filters_ref, wide_ref, twist_ref, mix_ref, ids_ref, embed_ref,
    out_hbm, inputs_ref, values_ref, out_ref, sems,
):
    channels, length = filters_ref.shape
    outer = length // LANES
    norm = 1.0 / length
    for block in range(outer):
        values_ref[block * channels : (block + 1) * channels, :] = (
            filters_ref[:, block * LANES : (block + 1) * LANES] * norm
        )
    copies = []
    for which in range(channels // GROUP):
        columns = [
            values_ref[pl.ds(which * GROUP + k, outer, stride=channels), :] for k in range(GROUP)
        ]
        bins = group_rows(which, outer)
        even, odd = spread(columns, wide_ref, twist_ref, False)
        out_ref[bins, :LANES] = mm_packed(even, mix_ref[0])
        out_ref[bins, LANES:] = mm_packed(odd, mix_ref[1])
        copies += start_all([(out_ref.at[bins], out_hbm.at[bins])], sems, which)
    inputs_ref[...] = mm(token_picks(ids_ref[...], embed_ref.shape[0]), embed_ref[...]).astype(
        BF16
    )
    wait_all(copies)


def convolve(values_ref, spectrum_ref, tables, sign, arrivals):
    exact_ref, twist_ref, mix_ref, back_ref = tables
    outer = twist_ref.shape[0]
    channels = values_ref.shape[0] // outer
    for which in range(channels // GROUP):
        base = which * GROUP
        columns = [
            values_ref[pl.ds(base + k, outer, stride=channels), :] for k in range(GROUP)
        ]
        pieces = spread(columns, exact_ref, twist_ref, True)
        bins = [mm_packed(piece, mix_ref[half]) for half, piece in enumerate(pieces)]
        arrivals[which].wait()
        filt = spectrum_ref[group_rows(which, outer), :]
        pieces = []
        for half in range(2):
            own = filt[:, half * LANES : (half + 1) * LANES]
            far = turn(own)
            low = in_low(own)
            straight = jnp.where(low, own, far)
            crossed = jnp.where(low, -sign * far, sign * own)
            product = bins[half] * straight + turn(bins[half]) * crossed
            pieces.append(mm_packed(product, mix_ref[2 + half]))
        result = gather_back(*pieces, back_ref, twist_ref)
        for k in range(GROUP):
            values_ref[pl.ds(base + k, outer, stride=channels), :] = result[k]


def swap_blocks(parts):
    lane = lax.broadcasted_iota(jnp.int32, parts[0].shape, 1) // SIDE
    out = []
    for to in range(HALVES):
        total = None
        for source in range(HALVES):
            moved = parts[source]
            if source != to:
                moved = pltpu.roll(moved, ((source - to) * SIDE) % LANES, 1)
            total = moved if total is None else jnp.where(lane == source, moved, total)
        out.append(total)
    return out


def lane_span(chunk, width):
    span = width // CHUNKS
    return pl.ds(chunk * span, span)


def peer_span(chunk, peers):
    span = peers // CHUNKS
    return pl.ds(chunk * span, span)


def second_core():
    return lax.axis_index("dp") % 2 == 1


def send_kernel(
    ids_ref, embed_hbm, grad_hbm, weight_hbm, out_hbm,
    embed_ref, grad_ref, weight_ref, out_ref, sems,
):
    vocab, width = embed_hbm.shape
    tokens = ids_ref.shape[1]
    peers = out_ref.shape[0]
    copies = start_all([(weight_hbm, weight_ref), (grad_hbm, grad_ref)], sems, 2 * CHUNKS)
    for chunk in range(CHUNKS):
        lane = lane_span(chunk, width)
        copies += start_all([(embed_hbm.at[:, lane], embed_ref.at[:, lane])], sems, chunk)
    ids = ids_ref[...]
    high = ids // LANES
    spare = lax.broadcasted_iota(jnp.int32, (TAIL - SENT, tokens), 0)
    coded = jnp.where(spare == 0, high, ids - LANES * high).astype(F32)
    picks = token_picks(ids, vocab)
    late = second_core()
    sent = []
    wait_all(copies[:2])
    for chunk in range(CHUNKS):
        copies[2 + chunk].wait()
        blocks = width // LANES // CHUNKS
        for block in range(chunk * blocks, (chunk + 1) * blocks):
            lane = slice(block * LANES, (block + 1) * LANES)
            if block % 2 == 0:
                pair = slice(block * LANES, (block + 2) * LANES)
                upstream = grad_ref[:, pair].astype(F32) * mm(picks, embed_ref[:, pair])
            turned = upstream[:, (block % 2) * LANES : (block % 2 + 1) * LANES].T
            part = weight_ref[:, lane].astype(F32)
            parts = swap_blocks([part[8 * g : 8 * g + 8] for g in range(HALVES)])
            for k, piece in enumerate(parts):
                rows = [
                    turned[k * SIDE : (k + 1) * SIDE],
                    piece[:4],
                    jnp.where(late, piece[6:8], piece[4:6]),
                    coded,
                ]
                out_ref[block * HALVES + k] = jnp.concatenate(rows, axis=0).astype(BF16)
        rows = peer_span(chunk, peers)
        sent += start_all([(out_ref.at[rows], out_hbm.at[rows])], sems, CHUNKS + chunk)
    wait_all(sent)


def read_ids(tails_ref, first):
    start = pl.multiple_of(first * TAIL, 2 * TAIL)
    tails = tails_ref[pl.ds(start, 2 * TAIL), :].astype(F32)
    both = jnp.concatenate([tails[SENT:TAIL], tails[TAIL + SENT :]], axis=1)
    high, low = both[0:1], both[1:2]
    index = lax.broadcasted_iota(jnp.int32, (LANES, 2 * LANES), 0).astype(F32)
    return high, jnp.where(index == low, 1.0, 0.0).astype(BF16)


def forward_kernel(
    tails_hbm, other_hbm, embed_hbm, spectrum_hbm, exact_hbm, twist_hbm, mix_hbm, back_hbm,
    out_hbm,
    tails_ref, other_ref, embed_ref, spectrum_ref, exact_ref, twist_ref, mix_ref, back_ref,
    values_ref, weight_ref, table_ref, out_ref, sems,
):
    peers = tails_ref.shape[0] // TAIL
    vocab, width = embed_ref.shape
    groups = SIDE // GROUP
    half = width // 2
    tails_copy, other_copy, embed_first, embed_second = start_all(
        [
            (tails_hbm, tails_ref),
            (other_hbm, other_ref),
            (embed_hbm.at[:, pl.ds(0, half)], embed_ref.at[:, pl.ds(0, half)]),
            (embed_hbm.at[:, pl.ds(half, half)], embed_ref.at[:, pl.ds(half, half)]),
        ],
        sems,
    )
    table_copies = start_all(
        [
            (exact_hbm, exact_ref),
            (twist_hbm, twist_ref),
            (mix_hbm, mix_ref),
            (back_hbm, back_ref),
        ],
        sems,
        4,
    )
    spectrum_copies = start_all(
        [
            (spectrum_hbm.at[group_rows(k, peers)], spectrum_ref.at[group_rows(k, peers)])
            for k in range(groups)
        ],
        sems,
        4 + TABLES,
    )
    tails_copy.wait()
    other_copy.wait()
    late = second_core()

    @pl.loop(0, peers // STEP)
    def _(step):
        others = other_ref[pl.ds(pl.multiple_of(step * 2 * STEP, 2 * STEP), 2 * STEP), :]
        others = others.astype(F32)
        tails = tails_ref[pl.ds(pl.multiple_of(step * TAIL * STEP, TAIL * STEP), TAIL * STEP), :]
        tails = tails.astype(F32)
        for k in range(STEP):
            peer = step * STEP + k
            tail = tails[k * TAIL : (k + 1) * TAIL]
            mine, other = tail[4:SENT], others[2 * k : 2 * k + 2]
            part = jnp.concatenate(
                [tail[:4], jnp.where(late, other, mine), jnp.where(late, mine, other)], axis=0
            )
            lane = lax.broadcasted_iota(jnp.int32, part.shape, 1) // SIDE
            rows = [jnp.where(lane == g, part, 0.0) for g in range(HALVES)]
            weight_ref[pl.ds(pl.multiple_of(peer * SIDE, SIDE), SIDE), :] = jnp.concatenate(
                rows, axis=0
            ).astype(BF16)

    embed_first.wait()
    table = mm(embed_ref[:, :half], weight_ref[:half])
    embed_second.wait()
    table = table + mm(embed_ref[:, half:], weight_ref[half:])
    table = table + pltpu.roll(table, 2 * SIDE, 1)
    table = table + pltpu.roll(table, SIDE, 1)
    parts = []
    for part in range(vocab // LANES):
        turned = table[part * LANES : (part + 1) * LANES].T
        parts.append(turned[:SIDE])
    table_ref[...] = jnp.concatenate(parts, axis=0).astype(BF16)

    @pl.loop(0, peers // STEP)
    def _(step):
        for k in range(0, STEP, 2):
            first = step * STEP + k
            high, picks = read_ids(tails_ref, first)
            every = mm(table_ref[...], picks)
            columns = every[:SIDE]
            for part in range(1, vocab // LANES):
                columns = jnp.where(
                    high == part, every[part * SIDE : (part + 1) * SIDE], columns
                )
            rows = jnp.concatenate([columns[:, :LANES], columns[:, LANES:]], axis=0)
            values_ref[pl.ds(pl.multiple_of(first * SIDE, 2 * SIDE), 2 * SIDE), :] = rows

    wait_all(table_copies)
    convolve(
        values_ref, spectrum_ref, (exact_ref, twist_ref, mix_ref, back_ref), 1.0, spectrum_copies
    )
    span = peers // CHUNKS
    copies = []
    for chunk in range(CHUNKS):
        rows = pl.ds(chunk * span, span)
        out_ref[rows] = (
            values_ref[pl.ds(chunk * span * SIDE, span * SIDE), :]
            .astype(BF16)
            .reshape(span, SIDE, LANES)
        )
        copies += start_all([(out_ref.at[rows], out_hbm.at[rows])], sems, 4 + TABLES + groups + chunk)
    wait_all(copies)


def backward_kernel(
    block_ref, embed_hbm, spectrum_hbm, exact_hbm, twist_hbm, mix_hbm, back_hbm,
    out_hbm, other_hbm, tails_hbm,
    embed_ref, spectrum_ref, exact_ref, twist_ref, mix_ref, back_ref,
    values_ref, sums_ref, out_ref, other_ref, tails_ref, sems,
):
    peers = block_ref.shape[0]
    vocab, width = embed_ref.shape
    groups = SIDE // GROUP
    scaling = 1.0 / math.sqrt(peers * LANES)
    table_copies = start_all(
        [
            (exact_hbm, exact_ref),
            (twist_hbm, twist_ref),
            (mix_hbm, mix_ref),
            (back_hbm, back_ref),
        ],
        sems,
    )
    spectrum_copies = start_all(
        [
            (spectrum_hbm.at[group_rows(k, peers)], spectrum_ref.at[group_rows(k, peers)])
            for k in range(groups)
        ],
        sems,
        1 + TABLES,
    )
    (embed_copy,) = start_all([(embed_hbm, embed_ref)], sems, 1 + TABLES + groups)

    @pl.loop(0, peers // STEP)
    def _(step):
        others, tails = [], []
        for k in range(STEP):
            peer = step * STEP + k
            part = block_ref[peer].astype(F32)
            values_ref[pl.ds(pl.multiple_of(peer * SIDE, SIDE), SIDE), :] = part[:SIDE]
            others.append(part[SIDE + 4 : SIDE + SENT])
            tails.append(part[SIDE:])
        other_ref[pl.ds(pl.multiple_of(step * 2 * STEP, 2 * STEP), 2 * STEP), :] = (
            jnp.concatenate(others, axis=0).astype(BF16)
        )
        tails_ref[pl.ds(pl.multiple_of(step * TAIL * STEP, TAIL * STEP), TAIL * STEP), :] = (
            jnp.concatenate(tails, axis=0).astype(BF16)
        )

    copies = start_all(
        [(other_ref, other_hbm), (tails_ref, tails_hbm)], sems, 2 + TABLES + groups
    )
    wait_all(table_copies)
    convolve(
        values_ref, spectrum_ref, (exact_ref, twist_ref, mix_ref, back_ref), -1.0, spectrum_copies
    )
    sums_ref[...] = jnp.zeros_like(sums_ref)

    @pl.loop(0, peers // STEP)
    def _(step):
        total = sums_ref[...]
        for k in range(0, STEP, 2):
            first = step * STEP + k
            high, picks = read_ids(tails_ref, first)
            rows = values_ref[pl.ds(pl.multiple_of(first * SIDE, 2 * SIDE), 2 * SIDE), :]
            columns = jnp.concatenate([rows[:SIDE], rows[SIDE:]], axis=1).astype(BF16)
            masked = [
                columns * jnp.where(high == part, 1.0, 0.0).astype(BF16)
                for part in range(vocab // LANES)
            ]
            total = total + lax.dot_general(
                jnp.concatenate(masked, axis=0),
                picks,
                (((1,), (1,)), ((), ())),
                preferred_element_type=F32,
            )
        sums_ref[...] = total

    sums = sums_ref[...]
    sums = jnp.concatenate(
        [sums[part * SIDE : (part + 1) * SIDE] for part in range(vocab // LANES)], axis=1
    )
    both = jnp.concatenate(halves(sums), axis=0)
    embed_copy.wait()
    blocks = width // LANES // CHUNKS
    for chunk in range(CHUNKS):
        for first in range(chunk * blocks, (chunk + 1) * blocks, 2):
            pair = mm(both, embed_ref[:, first * LANES : (first + 2) * LANES])
            pair = (pair[:SIDE] + pair[SIDE:]) * scaling
            for block in range(first, first + 2):
                lane = slice((block - first) * LANES, (block - first + 1) * LANES)
                grad = pair[:, lane]
                shifted = [grad] + [pltpu.roll(grad, LANES - 8 * g, 1) for g in range(1, HALVES)]
                turned = jnp.concatenate(shifted, axis=0).T
                for k in range(HALVES):
                    out_ref[block * HALVES + k] = turned[k * SIDE : k * SIDE + 8]
        rows = pl.ds(chunk * blocks * HALVES, blocks * HALVES)
        copies += start_all([(out_ref.at[rows], out_hbm.at[rows])], sems, 4 + TABLES + groups + chunk)
    wait_all(copies)


def momentum_kernel(
    grad_hbm, momentum_hbm, feedback_hbm, updated_hbm, residue_hbm, quant_hbm,
    grad_ref, updated_ref, total_ref, quant_ref, sems,
):
    peers = grad_ref.shape[0]
    width = total_ref.shape[1]
    blocks = width // LANES // CHUNKS
    copies = []
    for chunk in range(CHUNKS):
        lane = lane_span(chunk, width)
        rows = peer_span(chunk, peers)
        pairs = [
            (grad_hbm.at[rows], grad_ref.at[rows]),
            (momentum_hbm.at[:, lane], updated_ref.at[:, lane]),
            (feedback_hbm.at[:, lane], total_ref.at[:, lane]),
        ]
        copies.append(start_all(pairs, sems, 3 * chunk))
    sent = []
    weight = 0.0
    for chunk in range(CHUNKS):
        wait_all(copies[chunk])
        for block in range(chunk * blocks, (chunk + 1) * blocks):
            lane = slice(block * LANES, (block + 1) * LANES)
            parts = swap_blocks([grad_ref[block * HALVES + k] for k in range(HALVES)])
            grad = jnp.concatenate(parts, axis=0)
            updated = momentum_keep * updated_ref[:, lane] + (1.0 - momentum_keep) * grad
            updated_ref[:, lane] = updated
            total = updated + total_ref[:, lane]
            total_ref[:, lane] = total
            weight = weight + jnp.abs(total)
        lane = lane_span(chunk, width)
        sent += start_all(
            [(updated_ref.at[:, lane], updated_hbm.at[:, lane])], sems, 3 * CHUNKS + chunk
        )
    scale = jnp.sum(weight, axis=1, keepdims=True) / width + tiny_shift
    for chunk in range(CHUNKS):
        for block in range(chunk * blocks, (chunk + 1) * blocks):
            lane = slice(block * LANES, (block + 1) * LANES)
            total = total_ref[:, lane]
            quantized = (scale * jnp.clip(total / scale, -1.0, 1.0)).astype(BF16)
            quant_ref[:, lane] = quantized
            total_ref[:, lane] = total - quantized.astype(F32)
        lane = lane_span(chunk, width)
        pairs = [
            (quant_ref.at[:, lane], quant_hbm.at[:, lane]),
            (total_ref.at[:, lane], residue_hbm.at[:, lane]),
        ]
        sent += start_all(pairs, sems, 4 * CHUNKS + 2 * chunk)
    wait_all(sent)


def output_kernel(conv_ref, inputs_hbm, out_hbm, inputs_ref, out_ref, sems):
    width = out_ref.shape[1]
    blocks = width // LANES // CHUNKS
    copies = []
    for chunk in range(CHUNKS):
        lane = lane_span(chunk, width)
        copies += start_all([(inputs_hbm.at[:, lane], inputs_ref.at[:, lane])], sems, chunk)
    sent = []
    for chunk in range(CHUNKS):
        copies[chunk].wait()
        for block in range(chunk * blocks, (chunk + 1) * blocks):
            lane = slice(block * LANES, (block + 1) * LANES)
            rows = [conv_ref[block * HALVES + k].astype(F32) for k in range(HALVES)]
            conv = jnp.concatenate(rows, axis=0).T
            out_ref[:, lane] = (inputs_ref[:, lane].astype(F32) * conv).astype(BF16)
        lane = lane_span(chunk, width)
        sent += start_all([(out_ref.at[:, lane], out_hbm.at[:, lane])], sems, CHUNKS + chunk)
    wait_all(sent)


def spaces(kinds):
    return [
        pl.BlockSpec(memory_space={"h": pltpu.HBM, "a": pl.ANY, "v": pltpu.VMEM}[kind])
        for kind in kinds
    ]


def call(kernel, out_shape, ins, outs, scratch=(), flops=0, moved=0, limit=60817408):
    out_specs = spaces(outs)
    return pl.pallas_call(
        kernel,
        out_shape=out_shape,
        in_specs=spaces(ins),
        out_specs=out_specs if len(outs) > 1 else out_specs[0],
        scratch_shapes=list(scratch),
        compiler_params=pltpu.CompilerParams(vmem_limit_bytes=limit),
        cost_estimate=pl.CostEstimate(flops=flops, bytes_accessed=moved, transcendentals=0),
    )


def exchange(values):
    return lax.all_to_all(values, "seq", split_axis=0, concat_axis=0, tiled=True)


def per_device(ids, embed, weight, filters, out_grad, momentum, feedback):
    parts = lax.axis_size("seq")
    replicas = lax.axis_size("dp")
    vocab, width = embed.shape
    tokens = ids.shape[1]
    channels = filters.shape[0]
    rows = channels * parts
    shape = jax.ShapeDtypeStruct
    tables = transform_tables(parts, tokens)
    convolve_tables = [tables[name] for name in ("exact", "twist", "mix", "back")]

    table_scratch = [
        pltpu.VMEM(table.shape, F32 if table.dtype == np.float32 else BF16)
        for table in convolve_tables
    ]
    groups = channels // GROUP

    block = call(
        send_kernel,
        shape((parts, SIDE + TAIL, tokens), BF16),
        "vhhh",
        "h",
        [
            pltpu.VMEM((vocab, width), BF16),
            pltpu.VMEM((tokens, width), BF16),
            pltpu.VMEM((weight.shape[0], width), BF16),
            pltpu.VMEM((parts, SIDE + TAIL, tokens), BF16),
            pltpu.SemaphoreType.DMA((2 * CHUNKS + 2,)),
        ],
        flops=2 * tokens * vocab * width,
        moved=5 << 20,
    )(ids, embed, out_grad[0], weight)
    block = exchange(block)
    spectrum, inputs = call(
        spectrum_kernel,
        (shape((rows, 2 * tokens), F32), shape((tokens, width), BF16)),
        "vvvvvv",
        "hv",
        [
            pltpu.VMEM((rows, tokens), F32),
            pltpu.VMEM((rows, 2 * tokens), F32),
            pltpu.SemaphoreType.DMA((groups,)),
        ],
        flops=5 << 30,
        moved=3 << 20,
        limit=16777216,
    )(filters, tables["wide"], tables["twist"], tables["mix"], ids, embed)
    gradient, other, tails = call(
        backward_kernel,
        (
            shape((parts, 8, tokens), F32),
            shape((2 * parts, tokens), BF16),
            shape((TAIL * parts, tokens), BF16),
        ),
        "vhhhhhh",
        "hhh",
        [
            pltpu.VMEM((vocab, width), BF16),
            pltpu.VMEM((rows, 2 * tokens), F32),
            *table_scratch,
            pltpu.VMEM((rows, tokens), F32),
            pltpu.VMEM((LANES, LANES), F32),
            pltpu.VMEM((parts, 8, tokens), F32),
            pltpu.VMEM((2 * parts, tokens), BF16),
            pltpu.VMEM((TAIL * parts, tokens), BF16),
            pltpu.SemaphoreType.DMA((4 + TABLES + groups + CHUNKS,)),
        ],
        flops=10 << 30,
        moved=6 << 20,
        limit=62820000,
    )(block, embed, spectrum, *convolve_tables)
    other = lax.ppermute(other, "dp", [(source, source ^ 1) for source in range(replicas)])
    gradient = exchange(gradient)
    convolved = call(
        forward_kernel,
        shape((parts, channels, tokens), BF16),
        "aahhhhhh",
        "h",
        [
            pltpu.VMEM((TAIL * parts, tokens), BF16),
            pltpu.VMEM((2 * parts, tokens), BF16),
            pltpu.VMEM((vocab, width), BF16),
            pltpu.VMEM((rows, 2 * tokens), F32),
            *table_scratch,
            pltpu.VMEM((rows, tokens), F32),
            pltpu.VMEM((width, LANES), BF16),
            pltpu.VMEM((LANES, LANES), BF16),
            pltpu.VMEM((parts, channels, tokens), BF16),
            pltpu.SemaphoreType.DMA((4 + TABLES + groups + CHUNKS,)),
        ],
        flops=10 << 30,
        moved=6 << 20,
        limit=60817408,
    )(tails, other, embed, spectrum, *convolve_tables)
    convolved = exchange(convolved)
    updated, residue, quantized = call(
        momentum_kernel,
        (
            shape((weight.shape[0], width), F32),
            shape((weight.shape[0], width), F32),
            shape((weight.shape[0], width), BF16),
        ),
        "ahh",
        "hhh",
        [
            pltpu.VMEM((parts, 8, tokens), F32),
            pltpu.VMEM((weight.shape[0], width), F32),
            pltpu.VMEM((weight.shape[0], width), F32),
            pltpu.VMEM((weight.shape[0], width), BF16),
            pltpu.SemaphoreType.DMA((6 * CHUNKS,)),
        ],
        flops=1 << 20,
        moved=2 << 20,
        limit=60817408,
    )(gradient, momentum[0], feedback[0])
    def swap(values, flip):
        return lax.ppermute(values, "dp", [(source, source ^ flip) for source in range(replicas)])

    across = swap(quantized, 2)
    beside = swap(quantized, 1)
    corner = swap(across, 1)
    summed = (quantized.astype(F32) + beside.astype(F32)) + (
        across.astype(F32) + corner.astype(F32)
    )
    new_weight = (weight.astype(F32) - step_rate * (summed / replicas)).astype(BF16)
    output = call(
        output_kernel,
        shape((tokens, width), BF16),
        "va",
        "h",
        [
            pltpu.VMEM((tokens, width), BF16),
            pltpu.VMEM((tokens, width), BF16),
            pltpu.SemaphoreType.DMA((2 * CHUNKS,)),
        ],
        flops=1 << 20,
        moved=2 << 20,
        limit=16777216,
    )(convolved, inputs)
    return (output[None], updated[None], residue[None], new_weight)


def solution(mesh):
    placed = (
        P("dp", "seq"),
        P(),
        P("seq", None),
        P("seq", None),
        P("dp", "seq", None),
        P("dp", "seq", None),
        P("dp", "seq", None),
    )
    return jax.shard_map(
        per_device,
        mesh=mesh,
        in_specs=placed,
        out_specs=(
            P("dp", "seq", None),
            P("dp", "seq", None),
            P("dp", "seq", None),
            P("seq", None),
        ),
        check_vma=False,
    )
```

```python
import functools
import math

import jax
import jax.numpy as jnp
import numpy as np
from jax import lax
from jax.experimental import pallas as pl
from jax.experimental.pallas import tpu as pltpu
from jax.sharding import PartitionSpec as P

momentum_keep = 0.9
step_rate = 0.02
tiny_shift = 1e-06

F32 = jnp.float32
BF16 = jnp.bfloat16
LANES = 128
GROUP = 16
STEP = 32
TAIL = 8
SENT = 6
HALVES = 4
SIDE = 32
CHUNKS = 2
TABLES = 4


def split_const(table):
    high = np.asarray(table, np.float32).astype(BF16)
    low = (table - high.astype(np.float64)).astype(np.float32).astype(BF16)
    return high, low


def packed_mix(table):
    high, low = split_const(
        np.block([[table.real, table.imag], [-table.imag, table.real]])
    )
    return np.block([[high, low], [high, np.zeros_like(low)]])


def transform_tables(outer, inner):
    total = outer * inner
    freq = np.arange(outer)[:, None] + 0.25
    first = np.exp(-2j * np.pi * freq * np.arange(outer)[None, :] / outer)
    twist = np.exp(-2j * np.pi * freq * np.arange(inner)[None, :] / total)
    half = inner // 2
    near, bins = np.arange(half)[:, None], 2 * np.arange(half)[None, :]
    even = np.exp(-2j * np.pi * (near * bins % inner) / inner)
    odd = np.exp(-2j * np.pi * (near * (bins + 1) % inner) / inner)
    stage = np.concatenate([first.real, first.imag], axis=0)
    high, low = split_const(stage)
    back_high, back_low = split_const(stage.T)
    mixes = [packed_mix(table) for table in (even, odd, even.conj().T, odd.conj().T)]
    return {
        "exact": np.concatenate([high, low], axis=1),
        "wide": np.concatenate([high, high, low], axis=1),
        "back": np.concatenate([back_high, back_high, back_low], axis=1),
        "twist": np.concatenate([twist.real, twist.imag], axis=1).astype(np.float32),
        "mix": np.stack(mixes),
    }


def mm(left, right):
    return jnp.dot(left, right, preferred_element_type=F32)


def halves(values):
    high = values.astype(BF16)
    return high, (values - high.astype(F32)).astype(BF16)


def mm_packed(values, table):
    both = mm(jnp.concatenate(halves(values), axis=1), table)
    return both[:, :LANES] + both[:, LANES:]


def turn(values):
    return pltpu.roll(values, LANES // 2, 1)


def in_low(values):
    return lax.broadcasted_iota(jnp.int32, values.shape, 1) < LANES // 2


def spread(columns, stage_ref, twist_ref, exact):
    real_twist = twist_ref[:, :LANES]
    imag_twist = twist_ref[:, LANES:]
    outer = real_twist.shape[0]
    evens, odds = [], []
    for first in range(0, len(columns), 2):
        pair = jnp.concatenate(columns[first : first + 2], axis=1)
        if exact:
            high = pair.astype(BF16)
            stack = jnp.concatenate([high, high], axis=0)
        else:
            high, low = halves(pair)
            stack = jnp.concatenate([high, low, high], axis=0)
        grid = mm(stage_ref[...], stack)
        for which in range(2):
            lane = slice(which * LANES, (which + 1) * LANES)
            real = grid[:outer, lane]
            imag = grid[outer:, lane]
            spun_real = real * real_twist - imag * imag_twist
            spun_imag = real * imag_twist + imag * real_twist
            far_real, far_imag = turn(spun_real), turn(spun_imag)
            low = in_low(spun_real)
            evens.append(jnp.where(low, spun_real + far_real, spun_imag + far_imag))
            odds.append(jnp.where(low, spun_real - far_real, far_imag - spun_imag))
    return jnp.concatenate(evens, axis=0), jnp.concatenate(odds, axis=0)


def gather_back(even, odd, back_ref, twist_ref):
    real_twist = twist_ref[:, :LANES]
    imag_twist = twist_ref[:, LANES:]
    outer = real_twist.shape[0]
    count = even.shape[0] // outer
    turned = []
    for which in range(count):
        rows = slice(which * outer, (which + 1) * outer)
        total, change = even[rows] + odd[rows], even[rows] - odd[rows]
        low = in_low(total)
        real = jnp.where(low, total, turn(change))
        imag = jnp.where(low, turn(total), change)
        turned.append(
            jnp.concatenate(
                [
                    real * real_twist + imag * imag_twist,
                    imag * real_twist - real * imag_twist,
                ],
                axis=0,
            )
        )
    columns = []
    for first in range(0, count, 2):
        high, low = halves(jnp.concatenate(turned[first : first + 2], axis=1))
        pair = mm(back_ref[...], jnp.concatenate([high, low, high], axis=0))
        columns += [pair[:, :LANES], pair[:, LANES:]]
    return columns


def start_all(pairs, sems, first=0):
    copies = [
        pltpu.make_async_copy(source, target, sems.at[first + which])
        for which, (source, target) in enumerate(pairs)
    ]
    for copy in copies:
        copy.start()
    return copies


def wait_all(copies):
    for copy in copies:
        copy.wait()


def group_rows(which, outer):
    return pl.ds(which * GROUP * outer, GROUP * outer)


def token_picks(ids, vocab):
    column = jnp.broadcast_to(ids.astype(F32), (LANES, ids.shape[1])).T
    lane_index = lax.broadcasted_iota(jnp.int32, column.shape, 1).astype(F32)
    return jnp.concatenate(
        [
            jnp.where(column == lane_index + first, 1.0, 0.0).astype(BF16)
            for first in range(0, vocab, LANES)
        ],
        axis=1,
    )


def spectrum_kernel(
    filters_ref, wide_ref, twist_ref, mix_ref, ids_ref, embed_ref,
    out_hbm, inputs_ref, values_ref, out_ref, sems,
):
    channels, length = filters_ref.shape
    outer = length // LANES
    norm = 1.0 / length
    for block in range(outer):
        values_ref[block * channels : (block + 1) * channels, :] = (
            filters_ref[:, block * LANES : (block + 1) * LANES] * norm
        )
    copies = []
    for which in range(channels // GROUP):
        columns = [
            values_ref[pl.ds(which * GROUP + k, outer, stride=channels), :] for k in range(GROUP)
        ]
        bins = group_rows(which, outer)
        even, odd = spread(columns, wide_ref, twist_ref, False)
        out_ref[bins, :LANES] = mm_packed(even, mix_ref[0])
        out_ref[bins, LANES:] = mm_packed(odd, mix_ref[1])
        copies += start_all([(out_ref.at[bins], out_hbm.at[bins])], sems, which)
    inputs_ref[...] = mm(token_picks(ids_ref[...], embed_ref.shape[0]), embed_ref[...]).astype(
        BF16
    )
    wait_all(copies)


def convolve(values_ref, spectrum_ref, tables, sign, arrivals):
    exact_ref, twist_ref, mix_ref, back_ref = tables
    outer = twist_ref.shape[0]
    channels = values_ref.shape[0] // outer
    for which in range(channels // GROUP):
        base = which * GROUP
        columns = [
            values_ref[pl.ds(base + k, outer, stride=channels), :] for k in range(GROUP)
        ]
        pieces = spread(columns, exact_ref, twist_ref, True)
        bins = [mm_packed(piece, mix_ref[half]) for half, piece in enumerate(pieces)]
        arrivals[which].wait()
        filt = spectrum_ref[group_rows(which, outer), :]
        pieces = []
        for half in range(2):
            own = filt[:, half * LANES : (half + 1) * LANES]
            far = turn(own)
            low = in_low(own)
            straight = jnp.where(low, own, far)
            crossed = jnp.where(low, -sign * far, sign * own)
            product = bins[half] * straight + turn(bins[half]) * crossed
            pieces.append(mm_packed(product, mix_ref[2 + half]))
        result = gather_back(*pieces, back_ref, twist_ref)
        for k in range(GROUP):
            values_ref[pl.ds(base + k, outer, stride=channels), :] = result[k]


def swap_blocks(parts):
    lane = lax.broadcasted_iota(jnp.int32, parts[0].shape, 1) // SIDE
    out = []
    for to in range(HALVES):
        total = None
        for source in range(HALVES):
            moved = parts[source]
            if source != to:
                moved = pltpu.roll(moved, ((source - to) * SIDE) % LANES, 1)
            total = moved if total is None else jnp.where(lane == source, moved, total)
        out.append(total)
    return out


def lane_span(chunk, width):
    span = width // CHUNKS
    return pl.ds(chunk * span, span)


def peer_span(chunk, peers):
    span = peers // CHUNKS
    return pl.ds(chunk * span, span)


def second_core():
    return lax.axis_index("dp") % 2 == 1


def send_kernel(
    ids_ref, embed_hbm, grad_hbm, weight_hbm, out_hbm,
    embed_ref, grad_ref, weight_ref, out_ref, sems,
):
    vocab, width = embed_hbm.shape
    tokens = ids_ref.shape[1]
    peers = out_ref.shape[0]
    copies = start_all([(weight_hbm, weight_ref), (grad_hbm, grad_ref)], sems, 2 * CHUNKS)
    for chunk in range(CHUNKS):
        lane = lane_span(chunk, width)
        copies += start_all([(embed_hbm.at[:, lane], embed_ref.at[:, lane])], sems, chunk)
    ids = ids_ref[...]
    high = ids // LANES
    spare = lax.broadcasted_iota(jnp.int32, (TAIL - SENT, tokens), 0)
    coded = jnp.where(spare == 0, high, ids - LANES * high).astype(F32)
    picks = token_picks(ids, vocab)
    late = second_core()
    sent = []
    wait_all(copies[:2])
    for chunk in range(CHUNKS):
        copies[2 + chunk].wait()
        blocks = width // LANES // CHUNKS
        for block in range(chunk * blocks, (chunk + 1) * blocks):
            lane = slice(block * LANES, (block + 1) * LANES)
            if block % 2 == 0:
                pair = slice(block * LANES, (block + 2) * LANES)
                upstream = grad_ref[:, pair].astype(F32) * mm(picks, embed_ref[:, pair])
            turned = upstream[:, (block % 2) * LANES : (block % 2 + 1) * LANES].T
            part = weight_ref[:, lane].astype(F32)
            parts = swap_blocks([part[8 * g : 8 * g + 8] for g in range(HALVES)])
            for k, piece in enumerate(parts):
                rows = [
                    turned[k * SIDE : (k + 1) * SIDE],
                    piece[:4],
                    jnp.where(late, piece[6:8], piece[4:6]),
                    coded,
                ]
                out_ref[block * HALVES + k] = jnp.concatenate(rows, axis=0).astype(BF16)
        rows = peer_span(chunk, peers)
        sent += start_all([(out_ref.at[rows], out_hbm.at[rows])], sems, CHUNKS + chunk)
    wait_all(sent)


def read_ids(tails_ref, first):
    start = pl.multiple_of(first * TAIL, 2 * TAIL)
    tails = tails_ref[pl.ds(start, 2 * TAIL), :].astype(F32)
    both = jnp.concatenate([tails[SENT:TAIL], tails[TAIL + SENT :]], axis=1)
    high, low = both[0:1], both[1:2]
    index = lax.broadcasted_iota(jnp.int32, (LANES, 2 * LANES), 0).astype(F32)
    return high, jnp.where(index == low, 1.0, 0.0).astype(BF16)


def forward_kernel(
    tails_hbm, other_hbm, embed_hbm, spectrum_hbm, exact_hbm, twist_hbm, mix_hbm, back_hbm,
    out_hbm,
    tails_ref, other_ref, embed_ref, spectrum_ref, exact_ref, twist_ref, mix_ref, back_ref,
    values_ref, weight_ref, table_ref, out_ref, sems,
):
    peers = tails_ref.shape[0] // TAIL
    vocab, width = embed_ref.shape
    groups = SIDE // GROUP
    half = width // 2
    tails_copy, other_copy, embed_first, embed_second = start_all(
        [
            (tails_hbm, tails_ref),
            (other_hbm, other_ref),
            (embed_hbm.at[:, pl.ds(0, half)], embed_ref.at[:, pl.ds(0, half)]),
            (embed_hbm.at[:, pl.ds(half, half)], embed_ref.at[:, pl.ds(half, half)]),
        ],
        sems,
    )
    table_copies = start_all(
        [
            (exact_hbm, exact_ref),
            (twist_hbm, twist_ref),
            (mix_hbm, mix_ref),
            (back_hbm, back_ref),
        ],
        sems,
        4,
    )
    spectrum_copies = start_all(
        [
            (spectrum_hbm.at[group_rows(k, peers)], spectrum_ref.at[group_rows(k, peers)])
            for k in range(groups)
        ],
        sems,
        4 + TABLES,
    )
    tails_copy.wait()
    other_copy.wait()
    late = second_core()

    @pl.loop(0, peers // STEP)
    def _(step):
        others = other_ref[pl.ds(pl.multiple_of(step * 2 * STEP, 2 * STEP), 2 * STEP), :]
        others = others.astype(F32)
        tails = tails_ref[pl.ds(pl.multiple_of(step * TAIL * STEP, TAIL * STEP), TAIL * STEP), :]
        tails = tails.astype(F32)
        for k in range(STEP):
            peer = step * STEP + k
            tail = tails[k * TAIL : (k + 1) * TAIL]
            mine, other = tail[4:SENT], others[2 * k : 2 * k + 2]
            part = jnp.concatenate(
                [tail[:4], jnp.where(late, other, mine), jnp.where(late, mine, other)], axis=0
            )
            lane = lax.broadcasted_iota(jnp.int32, part.shape, 1) // SIDE
            rows = [jnp.where(lane == g, part, 0.0) for g in range(HALVES)]
            weight_ref[pl.ds(pl.multiple_of(peer * SIDE, SIDE), SIDE), :] = jnp.concatenate(
                rows, axis=0
            ).astype(BF16)

    embed_first.wait()
    table = mm(embed_ref[:, :half], weight_ref[:half])
    embed_second.wait()
    table = table + mm(embed_ref[:, half:], weight_ref[half:])
    table = table + pltpu.roll(table, 2 * SIDE, 1)
    table = table + pltpu.roll(table, SIDE, 1)
    parts = []
    for part in range(vocab // LANES):
        turned = table[part * LANES : (part + 1) * LANES].T
        parts.append(turned[:SIDE])
    table_ref[...] = jnp.concatenate(parts, axis=0).astype(BF16)

    @pl.loop(0, peers // STEP)
    def _(step):
        for k in range(0, STEP, 2):
            first = step * STEP + k
            high, picks = read_ids(tails_ref, first)
            every = mm(table_ref[...], picks)
            columns = every[:SIDE]
            for part in range(1, vocab // LANES):
                columns = jnp.where(
                    high == part, every[part * SIDE : (part + 1) * SIDE], columns
                )
            rows = jnp.concatenate([columns[:, :LANES], columns[:, LANES:]], axis=0)
            values_ref[pl.ds(pl.multiple_of(first * SIDE, 2 * SIDE), 2 * SIDE), :] = rows

    wait_all(table_copies)
    convolve(
        values_ref, spectrum_ref, (exact_ref, twist_ref, mix_ref, back_ref), 1.0, spectrum_copies
    )
    span = peers // CHUNKS
    copies = []
    for chunk in range(CHUNKS):
        rows = pl.ds(chunk * span, span)
        out_ref[rows] = (
            values_ref[pl.ds(chunk * span * SIDE, span * SIDE), :]
            .astype(BF16)
            .reshape(span, SIDE, LANES)
        )
        copies += start_all([(out_ref.at[rows], out_hbm.at[rows])], sems, 4 + TABLES + groups + chunk)
    wait_all(copies)


def backward_kernel(
    block_ref, embed_hbm, spectrum_hbm, exact_hbm, twist_hbm, mix_hbm, back_hbm,
    out_hbm, other_hbm, tails_hbm,
    embed_ref, spectrum_ref, exact_ref, twist_ref, mix_ref, back_ref,
    values_ref, sums_ref, out_ref, other_ref, tails_ref, sems,
):
    peers = block_ref.shape[0]
    vocab, width = embed_ref.shape
    groups = SIDE // GROUP
    scaling = 1.0 / math.sqrt(peers * LANES)
    table_copies = start_all(
        [
            (exact_hbm, exact_ref),
            (twist_hbm, twist_ref),
            (mix_hbm, mix_ref),
            (back_hbm, back_ref),
        ],
        sems,
    )
    spectrum_copies = start_all(
        [
            (spectrum_hbm.at[group_rows(k, peers)], spectrum_ref.at[group_rows(k, peers)])
            for k in range(groups)
        ],
        sems,
        1 + TABLES,
    )
    (embed_copy,) = start_all([(embed_hbm, embed_ref)], sems, 1 + TABLES + groups)

    @pl.loop(0, peers // STEP)
    def _(step):
        others, tails = [], []
        for k in range(STEP):
            peer = step * STEP + k
            part = block_ref[peer].astype(F32)
            values_ref[pl.ds(pl.multiple_of(peer * SIDE, SIDE), SIDE), :] = part[:SIDE]
            others.append(part[SIDE + 4 : SIDE + SENT])
            tails.append(part[SIDE:])
        other_ref[pl.ds(pl.multiple_of(step * 2 * STEP, 2 * STEP), 2 * STEP), :] = (
            jnp.concatenate(others, axis=0).astype(BF16)
        )
        tails_ref[pl.ds(pl.multiple_of(step * TAIL * STEP, TAIL * STEP), TAIL * STEP), :] = (
            jnp.concatenate(tails, axis=0).astype(BF16)
        )

    copies = start_all(
        [(other_ref, other_hbm), (tails_ref, tails_hbm)], sems, 2 + TABLES + groups
    )
    wait_all(table_copies)
    convolve(
        values_ref, spectrum_ref, (exact_ref, twist_ref, mix_ref, back_ref), -1.0, spectrum_copies
    )
    sums_ref[...] = jnp.zeros_like(sums_ref)

    @pl.loop(0, peers // STEP)
    def _(step):
        total = sums_ref[...]
        for k in range(0, STEP, 2):
            first = step * STEP + k
            high, picks = read_ids(tails_ref, first)
            rows = values_ref[pl.ds(pl.multiple_of(first * SIDE, 2 * SIDE), 2 * SIDE), :]
            columns = jnp.concatenate([rows[:SIDE], rows[SIDE:]], axis=1).astype(BF16)
            masked = [
                columns * jnp.where(high == part, 1.0, 0.0).astype(BF16)
                for part in range(vocab // LANES)
            ]
            total = total + lax.dot_general(
                jnp.concatenate(masked, axis=0),
                picks,
                (((1,), (1,)), ((), ())),
                preferred_element_type=F32,
            )
        sums_ref[...] = total

    sums = sums_ref[...]
    sums = jnp.concatenate(
        [sums[part * SIDE : (part + 1) * SIDE] for part in range(vocab // LANES)], axis=1
    )
    both = jnp.concatenate(halves(sums), axis=0)
    embed_copy.wait()
    blocks = width // LANES // CHUNKS
    for chunk in range(CHUNKS):
        for first in range(chunk * blocks, (chunk + 1) * blocks, 2):
            pair = mm(both, embed_ref[:, first * LANES : (first + 2) * LANES])
            pair = (pair[:SIDE] + pair[SIDE:]) * scaling
            for block in range(first, first + 2):
                lane = slice((block - first) * LANES, (block - first + 1) * LANES)
                grad = pair[:, lane]
                shifted = [grad] + [pltpu.roll(grad, LANES - 8 * g, 1) for g in range(1, HALVES)]
                turned = jnp.concatenate(shifted, axis=0).T
                for k in range(HALVES):
                    out_ref[block * HALVES + k] = turned[k * SIDE : k * SIDE + 8]
        rows = pl.ds(chunk * blocks * HALVES, blocks * HALVES)
        copies += start_all([(out_ref.at[rows], out_hbm.at[rows])], sems, 4 + TABLES + groups + chunk)
    wait_all(copies)


def momentum_kernel(
    grad_hbm, momentum_hbm, feedback_hbm, updated_hbm, residue_hbm, quant_hbm,
    grad_ref, updated_ref, total_ref, quant_ref, sems,
):
    peers = grad_ref.shape[0]
    width = total_ref.shape[1]
    blocks = width // LANES // CHUNKS
    copies = []
    for chunk in range(CHUNKS):
        lane = lane_span(chunk, width)
        rows = peer_span(chunk, peers)
        pairs = [
            (grad_hbm.at[rows], grad_ref.at[rows]),
            (momentum_hbm.at[:, lane], updated_ref.at[:, lane]),
            (feedback_hbm.at[:, lane], total_ref.at[:, lane]),
        ]
        copies.append(start_all(pairs, sems, 3 * chunk))
    sent = []
    weight = 0.0
    for chunk in range(CHUNKS):
        wait_all(copies[chunk])
        for block in range(chunk * blocks, (chunk + 1) * blocks):
            lane = slice(block * LANES, (block + 1) * LANES)
            parts = swap_blocks([grad_ref[block * HALVES + k] for k in range(HALVES)])
            grad = jnp.concatenate(parts, axis=0)
            updated = momentum_keep * updated_ref[:, lane] + (1.0 - momentum_keep) * grad
            updated_ref[:, lane] = updated
            total = updated + total_ref[:, lane]
            total_ref[:, lane] = total
            weight = weight + jnp.abs(total)
        lane = lane_span(chunk, width)
        sent += start_all(
            [(updated_ref.at[:, lane], updated_hbm.at[:, lane])], sems, 3 * CHUNKS + chunk
        )
    scale = jnp.sum(weight, axis=1, keepdims=True) / width + tiny_shift
    for chunk in range(CHUNKS):
        for block in range(chunk * blocks, (chunk + 1) * blocks):
            lane = slice(block * LANES, (block + 1) * LANES)
            total = total_ref[:, lane]
            quantized = (scale * jnp.clip(total / scale, -1.0, 1.0)).astype(BF16)
            quant_ref[:, lane] = quantized
            total_ref[:, lane] = total - quantized.astype(F32)
        lane = lane_span(chunk, width)
        pairs = [
            (quant_ref.at[:, lane], quant_hbm.at[:, lane]),
            (total_ref.at[:, lane], residue_hbm.at[:, lane]),
        ]
        sent += start_all(pairs, sems, 4 * CHUNKS + 2 * chunk)
    wait_all(sent)


def output_kernel(conv_ref, inputs_hbm, out_hbm, inputs_ref, out_ref, sems):
    width = out_ref.shape[1]
    blocks = width // LANES // CHUNKS
    copies = []
    for chunk in range(CHUNKS):
        lane = lane_span(chunk, width)
        copies += start_all([(inputs_hbm.at[:, lane], inputs_ref.at[:, lane])], sems, chunk)
    sent = []
    for chunk in range(CHUNKS):
        copies[chunk].wait()
        for block in range(chunk * blocks, (chunk + 1) * blocks):
            lane = slice(block * LANES, (block + 1) * LANES)
            rows = [conv_ref[block * HALVES + k].astype(F32) for k in range(HALVES)]
            conv = jnp.concatenate(rows, axis=0).T
            out_ref[:, lane] = (inputs_ref[:, lane].astype(F32) * conv).astype(BF16)
        lane = lane_span(chunk, width)
        sent += start_all([(out_ref.at[:, lane], out_hbm.at[:, lane])], sems, CHUNKS + chunk)
    wait_all(sent)


def spaces(kinds):
    return [
        pl.BlockSpec(memory_space={"h": pltpu.HBM, "a": pl.ANY, "v": pltpu.VMEM}[kind])
        for kind in kinds
    ]


def call(kernel, out_shape, ins, outs, scratch=(), flops=0, moved=0, limit=60817408):
    out_specs = spaces(outs)
    return pl.pallas_call(
        kernel,
        out_shape=out_shape,
        in_specs=spaces(ins),
        out_specs=out_specs if len(outs) > 1 else out_specs[0],
        scratch_shapes=list(scratch),
        compiler_params=pltpu.CompilerParams(vmem_limit_bytes=limit),
        cost_estimate=pl.CostEstimate(flops=flops, bytes_accessed=moved, transcendentals=0),
    )


def exchange(values):
    return lax.all_to_all(values, "seq", split_axis=0, concat_axis=0, tiled=True)


def per_device(ids, embed, weight, filters, out_grad, momentum, feedback):
    parts = lax.axis_size("seq")
    replicas = lax.axis_size("dp")
    vocab, width = embed.shape
    tokens = ids.shape[1]
    channels = filters.shape[0]
    rows = channels * parts
    shape = jax.ShapeDtypeStruct
    tables = transform_tables(parts, tokens)
    convolve_tables = [tables[name] for name in ("exact", "twist", "mix", "back")]

    table_scratch = [
        pltpu.VMEM(table.shape, F32 if table.dtype == np.float32 else BF16)
        for table in convolve_tables
    ]
    groups = channels // GROUP

    block = call(
        send_kernel,
        shape((parts, SIDE + TAIL, tokens), BF16),
        "vhhh",
        "h",
        [
            pltpu.VMEM((vocab, width), BF16),
            pltpu.VMEM((tokens, width), BF16),
            pltpu.VMEM((weight.shape[0], width), BF16),
            pltpu.VMEM((parts, SIDE + TAIL, tokens), BF16),
            pltpu.SemaphoreType.DMA((2 * CHUNKS + 2,)),
        ],
        flops=2 * tokens * vocab * width,
        moved=5 << 20,
    )(ids, embed, out_grad[0], weight)
    block = exchange(block)
    spectrum, inputs = call(
        spectrum_kernel,
        (shape((rows, 2 * tokens), F32), shape((tokens, width), BF16)),
        "vvvvvv",
        "hv",
        [
            pltpu.VMEM((rows, tokens), F32),
            pltpu.VMEM((rows, 2 * tokens), F32),
            pltpu.SemaphoreType.DMA((groups,)),
        ],
        flops=5 << 30,
        moved=3 << 20,
        limit=16777216,
    )(filters, tables["wide"], tables["twist"], tables["mix"], ids, embed)
    gradient, other, tails = call(
        backward_kernel,
        (
            shape((parts, 8, tokens), F32),
            shape((2 * parts, tokens), BF16),
            shape((TAIL * parts, tokens), BF16),
        ),
        "vhhhhhh",
        "hhh",
        [
            pltpu.VMEM((vocab, width), BF16),
            pltpu.VMEM((rows, 2 * tokens), F32),
            *table_scratch,
            pltpu.VMEM((rows, tokens), F32),
            pltpu.VMEM((LANES, LANES), F32),
            pltpu.VMEM((parts, 8, tokens), F32),
            pltpu.VMEM((2 * parts, tokens), BF16),
            pltpu.VMEM((TAIL * parts, tokens), BF16),
            pltpu.SemaphoreType.DMA((4 + TABLES + groups + CHUNKS,)),
        ],
        flops=10 << 30,
        moved=6 << 20,
        limit=62820000,
    )(block, embed, spectrum, *convolve_tables)
    other = lax.ppermute(other, "dp", [(source, source ^ 1) for source in range(replicas)])
    gradient = exchange(gradient)
    convolved = call(
        forward_kernel,
        shape((parts, channels, tokens), BF16),
        "aahhhhhh",
        "h",
        [
            pltpu.VMEM((TAIL * parts, tokens), BF16),
            pltpu.VMEM((2 * parts, tokens), BF16),
            pltpu.VMEM((vocab, width), BF16),
            pltpu.VMEM((rows, 2 * tokens), F32),
            *table_scratch,
            pltpu.VMEM((rows, tokens), F32),
            pltpu.VMEM((width, LANES), BF16),
            pltpu.VMEM((LANES, LANES), BF16),
            pltpu.VMEM((parts, channels, tokens), BF16),
            pltpu.SemaphoreType.DMA((4 + TABLES + groups + CHUNKS,)),
        ],
        flops=10 << 30,
        moved=6 << 20,
        limit=60817408,
    )(tails, other, embed, spectrum, *convolve_tables)
    convolved = exchange(convolved)
    updated, residue, quantized = call(
        momentum_kernel,
        (
            shape((weight.shape[0], width), F32),
            shape((weight.shape[0], width), F32),
            shape((weight.shape[0], width), BF16),
        ),
        "ahh",
        "hhh",
        [
            pltpu.VMEM((parts, 8, tokens), F32),
            pltpu.VMEM((weight.shape[0], width), F32),
            pltpu.VMEM((weight.shape[0], width), F32),
            pltpu.VMEM((weight.shape[0], width), BF16),
            pltpu.SemaphoreType.DMA((6 * CHUNKS,)),
        ],
        flops=1 << 20,
        moved=2 << 20,
        limit=16777216,
    )(gradient, momentum[0], feedback[0])
    def swap(values, flip):
        return lax.ppermute(values, "dp", [(source, source ^ flip) for source in range(replicas)])

    across = swap(quantized, 2)
    beside = swap(quantized, 1)
    corner = swap(across, 1)
    summed = (quantized.astype(F32) + beside.astype(F32)) + (
        across.astype(F32) + corner.astype(F32)
    )
    new_weight = (weight.astype(F32) - step_rate * (summed / replicas)).astype(BF16)
    output = call(
        output_kernel,
        shape((tokens, width), BF16),
        "va",
        "h",
        [
            pltpu.VMEM((tokens, width), BF16),
            pltpu.VMEM((tokens, width), BF16),
            pltpu.SemaphoreType.DMA((2 * CHUNKS,)),
        ],
        flops=1 << 20,
        moved=2 << 20,
        limit=16777216,
    )(convolved, inputs)
    return (output[None], updated[None], residue[None], new_weight)


def solution(mesh):
    placed = (
        P("dp", "seq"),
        P(),
        P("seq", None),
        P("seq", None),
        P("dp", "seq", None),
        P("dp", "seq", None),
        P("dp", "seq", None),
    )
    return jax.shard_map(
        per_device,
        mesh=mesh,
        in_specs=placed,
        out_specs=(
            P("dp", "seq", None),
            P("dp", "seq", None),
            P("dp", "seq", None),
            P("seq", None),
        ),
        check_vma=False,
    )
```
